512 devices in a mesh: dp: 8 (over x, core), point: 64 (over y, z).
Axes of the slice: x: 4, y: 8, z: 8, core: 2. Of those that a mesh axis runs over, the one named last changes fastest.
Arguments:
- node_inputs_mapped: bfloat16 [8, 24576, 1024], P('dp', 'point'), as said below
- pooling_inputs: bfloat16 [8, 24576, 1024], P('dp', 'point'), may hold values from -6 to 6
- result_cotangent: bfloat16 [8, 24576, 1024], P('dp', 'point'), may hold values from -6 to 6
- partition_energy_map: bfloat16 [64, 64], replicated
- sharpness_factor: float32 [16], replicated, may hold values from 0.2 to 1
- centroid_linear_maps: float32 [64, 192], replicated, may hold values from -0.75 to 0.75
Outputs:
- layer_output: bfloat16 [8, 24576, 1024], P('dp', 'point')
- grad_mid: bfloat16 [8, 24576, 1024], P('dp', 'point')
- pooling_input_cotangent: bfloat16 [8, 24576, 1024], P('dp', 'point')
- grad_slice: float32 [64, 64], P('dp')
- grad_temp: float32 [16], P('dp')
- grad_token: float32 [64, 192], P('dp')
The draws below stay inside these ranges and needn't reach their ends.
Inputs may be any that keep to these rules, and one draw needn't show every extreme that they name: node_inputs_mapped is of order one in most rows; a few head vectors may be much larger.
All inputs are finite; a program needn't handle non-finite values.
Results may differ from the reference program's by a relative error of at most 0.012.
The reference program's roundings to bfloat16 on the way count: a program that leaves them out, or rounds other values in their place, can miss the bound.
Values sent between devices are 32-bit elements; how exact they have to be, the bound alone decides.
A program may use at most 64 MiB of HBM per device.

```python
import math
import jax
import jax.numpy as jnp
from jax import lax

NUM_GROUPS = 16
CHANNEL_WIDTH = 64
M = 64
REPLICAS = 8
POINTS = 24576


def slice_base(key):
    return jax.random.normal(key, (CHANNEL_WIDTH, M), jnp.float32) * CHANNEL_WIDTH ** (-0.5)


def draw_partition_energy_map(key, part):
    base = slice_base(key)
    return base.astype(jnp.bfloat16)


def draw_node_inputs_mapped(key, part):
    key = jax.random.fold_in(key, 12)
    first = jax.random.fold_in(key, 0)
    array_shape = (REPLICAS, POINTS, NUM_GROUPS, CHANNEL_WIDTH)
    values = jax.random.normal(first, array_shape, jnp.float32)
    return values.reshape(REPLICAS, POINTS, NUM_GROUPS * CHANNEL_WIDTH).astype(jnp.bfloat16)


def level_of(rng, shape, shards, smallest, largest):
    def one(position, blocks):
        steps = jax.random.uniform(jax.random.fold_in(jax.random.fold_in(rng, 6), position), (blocks,), jnp.float32, smallest / len(shards), largest / len(shards))
        return jnp.repeat(jnp.exp(steps), shape[position] // blocks).reshape((-1,) + (1,) * (len(shape) - position - 1))

    loudness = one(*shards[0])
    for cut in shards[1:]:
        loudness = loudness * one(*cut)
    return loudness


def centred(key, dims, deviation, reach, cuts=(), dtype=jnp.bfloat16):
    entries = jax.random.normal(key, dims, jnp.float32) * deviation
    if len(cuts) > 0:
        entries = level_of(key, dims, cuts, -0.22, 0.18) * entries
    return jnp.clip(entries, min=-reach, max=reach).astype(dtype)


def setup_inputs(seed: int = 0) -> dict:
    seeds = jax.random.split(jax.random.key(seed), 7)
    return {
        "node_inputs_mapped": draw_node_inputs_mapped(jax.random.fold_in(seeds[6], 71), 0),
        "pooling_inputs": centred(seeds[1], (REPLICAS, POINTS, NUM_GROUPS * CHANNEL_WIDTH), 1.0, 6.0, ((0, 8), (1, 64))),
        "result_cotangent": centred(seeds[2], (REPLICAS, POINTS, NUM_GROUPS * CHANNEL_WIDTH), 1.0, 6.0, ((0, 8), (1, 64))),
        "partition_energy_map": draw_partition_energy_map(jax.random.fold_in(seeds[6], 71), 0),
        "sharpness_factor": jnp.clip(jnp.exp(jax.random.uniform(seeds[4], (NUM_GROUPS,), jnp.float32, math.log(0.2), math.log(1.0))), 0.2, 1.0),
        "centroid_linear_maps": centred(seeds[5], (CHANNEL_WIDTH, 3 * CHANNEL_WIDTH), CHANNEL_WIDTH ** -0.5, 0.75, (), jnp.float32),
    }


epsilon = 1e-5
highest_precision = lax.Precision.HIGHEST


def lone_surface(node_tile, pooling_input_tile, upstream_cotangent_tile, partition_energy_map, sharpness_factor, centroid_linear_maps):
    tally_number = node_tile.shape[0]
    node_channel_groups = node_tile.reshape(tally_number, NUM_GROUPS, CHANNEL_WIDTH).astype(jnp.float32)
    feature_per_head = pooling_input_tile.reshape(tally_number, NUM_GROUPS, CHANNEL_WIDTH).astype(jnp.float32)
    gradient_per_head = upstream_cotangent_tile.reshape(tally_number, NUM_GROUPS, CHANNEL_WIDTH).astype(jnp.float32)
    sw32 = partition_energy_map.astype(jnp.float32)
    partition_energies = jnp.einsum('phd,dm->phm', node_channel_groups, sw32)
    partition_denominator = partition_energies / sharpness_factor[None, :, None]
    partition_assignment = jax.nn.softmax(partition_denominator, axis=-1)
    slice_bias = partition_assignment.astype(jnp.bfloat16).astype(jnp.float32)
    pooled_features = jnp.einsum('onw,onf->nwf', slice_bias, feature_per_head)
    mass = jnp.sum(partition_assignment, axis=0)
    inverse = 1.0 / (mass + epsilon)
    slice_token = pooled_features * inverse[..., None]
    projection = jnp.einsum('ugb,bp->ugp', slice_token, centroid_linear_maps, precision=highest_precision)
    query_tokens = projection[..., :CHANNEL_WIDTH]
    key_transposed = projection[..., CHANNEL_WIDTH:2 * CHANNEL_WIDTH]
    value_tokens = projection[..., 2 * CHANNEL_WIDTH:]
    score_scale = CHANNEL_WIDTH ** -0.5
    attention_score = jnp.einsum('sfv,siv->sfi', query_tokens, key_transposed, precision=highest_precision) * score_scale
    attention_probs = jax.nn.softmax(attention_score, axis=-1)
    mixed_tokens = jnp.einsum('lpx,lxw->lpw', attention_probs, value_tokens, precision=highest_precision)
    mixed_tokens_batch = mixed_tokens.astype(jnp.bfloat16).astype(jnp.float32)
    layer_output = jnp.einsum('zfi,fil->zfl', slice_bias, mixed_tokens_batch).astype(jnp.bfloat16)
    mixed_gradient = jnp.einsum('onw,onf->nwf', slice_bias, gradient_per_head)
    slice_gradient_1 = jnp.einsum('zgu,glu->zgl', gradient_per_head, mixed_tokens_batch)
    attention_probs_gradient = jnp.einsum('sfv,siv->sfi', mixed_gradient, value_tokens, precision=highest_precision)
    value_gradient = jnp.einsum('voi,voj->vij', attention_probs, mixed_gradient, precision=highest_precision)
    score_gradient = attention_probs * (attention_probs_gradient - jnp.sum(attention_probs * attention_probs_gradient, axis=-1, keepdims=True)) * score_scale
    query_gradient = jnp.einsum('lpx,lxw->lpw', score_gradient, key_transposed, precision=highest_precision)
    key_gradient = jnp.einsum('voi,voj->vij', score_gradient, query_tokens, precision=highest_precision)
    projection_gradient = jnp.concatenate([query_gradient, key_gradient, value_gradient], axis=-1)
    centroid_cotangent_entries = jnp.einsum('qtj,qtx->jx', slice_token, projection_gradient, precision=highest_precision)
    token_gradient = jnp.einsum('wfi,ki->wfk', projection_gradient, centroid_linear_maps, precision=highest_precision)
    grad_pool = token_gradient * inverse[..., None]
    mass_gradient = -jnp.sum(token_gradient * slice_token, axis=-1) * inverse
    pooled_batch_gradient = grad_pool.astype(jnp.bfloat16).astype(jnp.float32)
    pooling_input_cotangent = jnp.einsum('zfi,fil->zfl', slice_bias, pooled_batch_gradient).astype(jnp.bfloat16)
    slice_gradient_sum = slice_gradient_1 + jnp.einsum('zgu,glu->zgl', feature_per_head, pooled_batch_gradient) + mass_gradient[None]
    denominator_cotangent = partition_assignment * (slice_gradient_sum - jnp.sum(partition_assignment * slice_gradient_sum, axis=-1, keepdims=True))
    assignment_cotangent = denominator_cotangent / sharpness_factor[None, :, None]
    sharpness_cotangent_entries = -jnp.sum(denominator_cotangent * partition_denominator, axis=(0, 2)) / sharpness_factor
    grad_logit_b = assignment_cotangent.astype(jnp.bfloat16).astype(jnp.float32)
    grad_mid = jnp.einsum('phm,dm->phd', grad_logit_b, sw32).astype(jnp.bfloat16)
    partition_cotangent_local = jnp.einsum('phd,phm->dm', node_channel_groups, grad_logit_b)
    return (layer_output.reshape(tally_number, NUM_GROUPS * CHANNEL_WIDTH), grad_mid.reshape(tally_number, NUM_GROUPS * CHANNEL_WIDTH),
            pooling_input_cotangent.reshape(tally_number, NUM_GROUPS * CHANNEL_WIDTH), partition_cotangent_local, sharpness_cotangent_entries, centroid_cotangent_entries)


def reference(node_inputs_mapped, pooling_inputs, result_cotangent, partition_energy_map, sharpness_factor, centroid_linear_maps):
    def apply(entry_tile):
        return lone_surface(entry_tile[0], entry_tile[1], entry_tile[2], partition_energy_map, sharpness_factor, centroid_linear_maps)

    results = lax.map(apply, (node_inputs_mapped, pooling_inputs, result_cotangent))
    layer_output, grad_mid, pooling_input_cotangent, grad_slice, grad_temp, grad_token = results
    return (layer_output, grad_mid, pooling_input_cotangent, jnp.sum(grad_slice, axis=0),
            jnp.sum(grad_temp, axis=0), jnp.sum(grad_token, axis=0))
```

```python
import functools

import jax
import jax.numpy as jnp
from jax import lax
from jax.experimental import pallas as pl
from jax.experimental.pallas import tpu as pltpu
from jax.sharding import PartitionSpec as P

epsilon = 1e-05
f32 = jnp.float32
bf16 = jnp.bfloat16
W = 64
Q = 4
QW = Q * W
NN = (((1,), (0,)), ((), ()))
NT = (((1,), (1,)), ((), ()))


def bdot(a, b, dims=NN):
    return lax.dot_general(a, b, dims, preferred_element_type=f32)


def hdot(a, b, dims=NN):
    return lax.dot_general(
        a, b, dims, preferred_element_type=f32, precision=lax.Precision.HIGHEST
    )


def swap_halves(x):
    return pltpu.roll(x, W, 1)


def kernel(
    N,
    ND,
    H,
    node_h,
    pool_h,
    cot_h,
    w_ref,
    sharp_ref,
    maps_ref,
    lo_ref,
    gm_ref,
    pc_ref,
    gs_ref,
    gt_ref,
    gk_ref,
    node,
    pool,
    cot,
    zed,
    sl,
    slt,
    slb,
    glt,
    bt,
    mbs,
    gbs,
    send1,
    recv1,
    send2,
    recv2,
    tok,
    res,
    acc,
    tpart,
    tgrad,
    fin,
    tred,
    fred,
    in_sem,
    s1,
    r1,
    s2,
    r2,
    sg,
    rg,
    s3,
    r3,
    st,
    rt,
    sf,
    rf,
):
    QN = H // Q
    R2 = W // N
    R = W // ND
    PTS = node.shape[0]
    point = lax.axis_index("point")
    me_d = lax.axis_index("dp")
    me_y = point // N
    me_z = point % N

    def first(f):
        return jnp.where(f == 0, me_y, me_z) if not isinstance(f, int) else (me_y, me_z)[f]

    def second(f):
        return jnp.where(f == 0, me_z, me_y) if not isinstance(f, int) else (me_z, me_y)[f]

    def place(f, i, j):
        if isinstance(f, int):
            return i * N + j if f == 0 else j * N + i
        return jnp.where(f == 0, i * N + j, j * N + i)

    def rcopy(src, dst, ssem, rsem, **dev):
        return pltpu.make_async_remote_copy(
            src_ref=src,
            dst_ref=dst,
            send_sem=ssem,
            recv_sem=rsem,
            device_id=dev,
            device_id_type=pl.DeviceIdType.MESH,
        )

    barrier = pltpu.get_barrier_semaphore()
    for k in range(1, N):
        for dev in (place(0, (me_y + k) % N, me_z), place(0, me_y, (me_z + k) % N)):
            pl.semaphore_signal(
                barrier, inc=1, device_id={"point": dev}, device_id_type=pl.DeviceIdType.MESH
            )
    for k in range(1, ND):
        pl.semaphore_signal(
            barrier,
            inc=1,
            device_id={"dp": (me_d + k) % ND},
            device_id_type=pl.DeviceIdType.MESH,
        )

    def order(t):
        return (t % 2) * (QN // 2) + t // 2 if QN > 1 else t

    def fetch(q):
        lanes = pl.ds(pl.multiple_of(q * QW, QW), QW)
        return [
            pltpu.make_async_copy(s.at[0, :, lanes], d.at[:, lanes], in_sem.at[n, q])
            for n, (s, d) in enumerate(((node_h, node), (pool_h, pool), (cot_h, cot)))
        ]

    for t in range(QN):
        for c in fetch(order(t)):
            c.start()

    w4 = jnp.concatenate([w_ref[...].astype(f32)] * Q, axis=0)
    w4 = jnp.concatenate([w4] * Q, axis=1)
    row = lax.broadcasted_iota(jnp.int32, (QW, QW), 0)
    col = lax.broadcasted_iota(jnp.int32, (QW, QW), 1)
    w4 = jnp.where(row // W == col // W, w4, 0.0)
    bt[...] = w4.T.astype(bf16)
    lane = lax.broadcasted_iota(jnp.int32, (W, 2 * W), 1)
    low = lane < W
    low8 = low[:8]

    def inv_sharp(h, width):
        return 1.0 / jnp.full((1, width), sharp_ref[h], f32)

    def rows_of(q, i=0, n=QW):
        return pl.ds(pl.multiple_of(q * QW + i * W, W), n)

    def lanes_of(q):
        return pl.ds(pl.multiple_of(q * QW, QW), QW)

    def phase1(h):
        f, i = h // N, h % N
        return rcopy(
            send1.at[h],
            recv1.at[f, first(f)],
            s1.at[h],
            r1.at[f, first(f)],
            point=place(f, i, second(f)),
        )

    def forward(t, carry):
        q = order(t)
        for c in fetch(q):
            c.wait()
        z = bdot(bt[...], node[:, lanes_of(q)], NT)
        low_parts = []
        for i in range(Q):
            zh = z[i * W : (i + 1) * W] * inv_sharp(q * Q + i, PTS)
            e = jnp.exp(zh - jnp.max(zh, axis=0, keepdims=True))
            s = e * (1.0 / jnp.sum(e, axis=0, keepdims=True))
            sb = s.astype(bf16)
            zed[rows_of(q, i, W), :] = zh
            sl[rows_of(q, i, W), :] = s
            slt[rows_of(q, i, W), :] = sb
            low_parts.append((s - sb.astype(f32)).astype(bf16))
        sq = slt[rows_of(q), :]
        ones = jnp.ones((8, PTS), bf16)
        mass = bdot(ones, sq, NT) + bdot(ones, jnp.concatenate(low_parts, axis=0), NT)
        pooled = bdot(sq, pool[:, lanes_of(q)])
        gmixed = bdot(sq, cot[:, lanes_of(q)])
        for i in range(Q):
            r, c = slice(i * W, (i + 1) * W), slice(i // 2 * 2 * W, (i // 2 + 1) * 2 * W)
            a, b, m = pooled[r, c], gmixed[r, c], mass[:, c]
            if i % 2 == 0:
                b = swap_halves(b)
            else:
                a, m = swap_halves(a), swap_halves(m)
            send1[q * Q + i, :W, :] = jnp.where(low, a, b)
            send1[q * Q + i, W:, :] = m

        @pl.when(t == 0)
        def _():
            pl.semaphore_wait(barrier, 2 * (N - 1) + ND - 1)

        for i in range(Q):
            h = q * Q + i

            @pl.when(h % N != first(h // N))
            def _():
                phase1(h).start()

        return carry

    lax.fori_loop(0, QN, forward, 0)

    def flip(q):
        slb[:, lanes_of(q)] = slt[rows_of(q), :].T

    for q in range(QN):
        flip(q)

    def phase2(f, j):
        return rcopy(
            send2.at[f, j],
            recv2.at[f, second(f)],
            s2.at[f, j],
            r2.at[f, second(f)],
            point=place(f, first(f), j),
        )

    for f in range(2):
        recv1[f, first(f)] = send1[f * N + first(f)]
        for k in range(1, N):
            i = (first(f) + k) % N
            rcopy(
                send1.at[0], recv1.at[f, i], s1.at[0], r1.at[f, i], point=place(f, i, second(f))
            ).wait_recv()
        part = recv1[f, 0]
        for i in range(1, N):
            part = part + recv1[f, i]
        for j in range(N):
            send2[f, j, :R2, :] = part[j * R2 : (j + 1) * R2]
            send2[f, j, R2:, :] = part[W:]
        for k in range(1, N):
            phase2(f, (second(f) + k) % N).start()
        recv2[f, second(f)] = send2[f, second(f)]

    def gather2(f, j):
        mine = tok.at[f, pl.ds(pl.multiple_of(second(f) * R2, R2), R2)]
        return rcopy(
            mine, mine, sg.at[f, j], rg.at[f, second(f)], point=place(f, first(f), j)
        )

    masses = []
    for f in range(2):
        for k in range(1, N):
            j = (second(f) + k) % N
            rcopy(
                send2.at[f, j], recv2.at[f, j], s2.at[f, j], r2.at[f, j], point=place(f, first(f), j)
            ).wait_recv()
        total = recv2[f, 0]
        for j in range(1, N):
            total = total + recv2[f, j]
        tok[f, pl.ds(pl.multiple_of(second(f) * R2, R2), R2), :] = total[:R2]
        for k in range(1, N):
            gather2(f, (second(f) + k) % N).start()
        masses.append(total[R2:])

    for q in range(QN):
        mbs[q] = jnp.zeros((QW, QW), bf16)
        gbs[q] = jnp.zeros((QW, QW), bf16)
    acc[...] = jnp.zeros(acc.shape, f32)

    maps = maps_ref[...]

    def phase3(f, i):
        h = f * N + first(f)
        return rcopy(
            res.at[h], res.at[h], s3.at[f, i], r3.at[h], point=place(f, i, second(f))
        )

    token_grads = []
    for f in range(2):
        for k in range(1, N):
            j = (second(f) + k) % N
            theirs = tok.at[f, pl.ds(pl.multiple_of(j * R2, R2), R2)]
            rcopy(
                theirs, theirs, sg.at[f, j], rg.at[f, j], point=place(f, first(f), j)
            ).wait_recv()
    for f in range(2):
        both = tok[f]
        inverse = (1.0 / (masses[f] + epsilon)).T[:W, :1]
        t = both[:, :W] * inverse
        gmix = swap_halves(both)[:, :W]
        proj = hdot(t, maps)
        query, key, value = proj[:, :W], swap_halves(proj[:, : 2 * W])[:, :W], proj[:, 2 * W :]
        score = hdot(query, key, NT) * W**-0.5
        e = jnp.exp(score - jnp.max(score, axis=1, keepdims=True))
        attn = e / jnp.sum(e, axis=1, keepdims=True)
        mixed = hdot(attn, value)
        gattn = hdot(gmix, value, NT)
        gvalue = hdot(attn.T, gmix)
        gscore = attn * (gattn - jnp.sum(attn * gattn, axis=1, keepdims=True)) * W**-0.5
        gquery = hdot(gscore, key)
        gkey = hdot(gscore.T, query)
        gproj = jnp.concatenate([gquery, gkey, gvalue], axis=1)
        gtok = hdot(gproj, maps, NT)
        gpool = gtok * inverse
        gmass = hdot(jnp.ones((8, W), f32), -(gtok * t) * inverse, NT)
        h = f * N + first(f)
        res[h, :W, :] = jnp.concatenate(
            [mixed.astype(bf16).astype(f32), gpool.astype(bf16).astype(f32)], axis=1
        )
        zero8 = jnp.zeros((8, W), f32)
        res[h, W:, :] = jnp.where(
            (jnp.zeros((8, 2 * W), jnp.int32) + h) % 2 == 0,
            jnp.concatenate([gmass, zero8], axis=1),
            jnp.concatenate([zero8, gmass], axis=1),
        )
        for k in range(1, N):
            phase3(f, (first(f) + k) % N).start()
        token_grads.append(hdot(t.T, gproj))

    def all_of(buf, ssem, rsem):
        axes = ((me_d, ND), (me_z, N), (me_y, N))

        def dev(stage, k):
            if stage == 0:
                return {"dp": k}
            return {"point": place(0, me_y, k) if stage == 1 else place(0, k, me_z)}

        def copy(stage, k, src):
            me = axes[stage][0]
            return rcopy(
                src, buf.at[stage, me], ssem.at[stage, k], rsem.at[stage, me], **dev(stage, k)
            )

        def send(stage, source):
            me, n = axes[stage]
            for k in range(1, n):
                k = (me + k) % n
                copy(stage, k, source(k)).start()

        def receive(stage):
            me, n = axes[stage]
            for k in range(1, n):
                k = (me + k) % n
                rcopy(
                    buf.at[stage, k],
                    buf.at[stage, k],
                    ssem.at[stage, k],
                    rsem.at[stage, k],
                    **dev(stage, k),
                ).wait_recv()
            total = buf[stage, 0]
            for k in range(1, n):
                total = total + buf[stage, k]
            return total

        def begin(source):
            buf[0, me_d] = source[me_d]
            send(0, lambda k: source.at[k])

        def onward(stage):
            total = receive(stage - 1)
            me = axes[stage][0]
            buf[stage, me] = total
            send(stage, lambda k: buf.at[stage, me])

        def finish():
            return receive(2)

        def drain():
            for stage in range(3):
                me, n = axes[stage]
                for k in range(1, n):
                    k = (me + k) % n
                    copy(stage, k, buf.at[stage, me]).wait_send()

        return begin, onward, finish, drain

    t_begin, t_onward, t_finish, t_drain = all_of(tred, st, rt)
    f_begin, f_onward, f_finish, f_drain = all_of(fred, sf, rf)

    tg = (token_grads[0] + token_grads[1]) * (1.0 / N)
    tg = jnp.concatenate([tg, jnp.zeros((W, W), f32)], axis=1)
    for d in range(ND):
        tgrad[d] = tg[d * R : (d + 1) * R]
    t_begin(tgrad)

    def backward(t, carry):
        q = order(t)
        for i in range(Q):
            h = q * Q + i
            f = h // N

            @pl.when(h % N != first(f))
            def _():
                rcopy(
                    res.at[h], res.at[h], s3.at[0, 0], r3.at[h], point=place(f, h % N, second(f))
                ).wait_recv()

        cols = []
        for i in range(Q):
            c = slice(i // 2 * 2 * W, (i // 2 + 1) * 2 * W)
            r = slice(i * W, (i + 1) * W)
            both = res[q * Q + i, :W, :]
            other = swap_halves(both)
            m, g = (both, other) if i % 2 == 0 else (other, both)
            keep = low if i % 2 == 0 else ~low
            mbs[q, r, c] = jnp.where(keep, m, 0.0).astype(bf16)
            gbs[q, r, c] = jnp.where(keep, g, 0.0).astype(bf16)
            if i % 2 == 0:
                cols.append((res[q * Q + i, W:, :] + res[q * Q + i + 1, W:, :]).T[:, :1])
        gq = bdot(mbs[q], cot[:, lanes_of(q)], NT) + bdot(gbs[q], pool[:, lanes_of(q)], NT)
        for i in range(Q):
            h = q * Q + i
            s = sl[rows_of(q, i, W), :]
            g = gq[i * W : (i + 1) * W] + cols[i // 2][i % 2 * W : (i % 2 + 1) * W]
            sg_ = s * g
            gz = sg_ - s * jnp.sum(sg_, axis=0, keepdims=True)
            glt[rows_of(q, i, W), :] = (gz * inv_sharp(h, PTS)).astype(bf16)
            tz = gz * zed[rows_of(q, i, W), :]
            tpart[h] = jnp.sum(tz.reshape(W // 8, 8, PTS), axis=0)
        gs = bdot(glt[rows_of(q), :], node[:, lanes_of(q)])
        for i in range(Q):
            c = slice(i // 2 * 2 * W, (i // 2 + 1) * 2 * W)
            acc[i % 2] += gs[i * W : (i + 1) * W, c]
        return carry

    lax.fori_loop(0, QN, backward, 0)
    t_onward(1)

    gst = jnp.where(low, acc[0] + swap_halves(acc[1]), 0.0)
    gst = jnp.concatenate([gst, jnp.zeros((W, 2 * W), f32)], axis=0).T[:W]
    temps = []
    for h in range(H):
        v = jnp.sum(jnp.sum(tpart[h], axis=0, keepdims=True), axis=1, keepdims=True)
        temps.append(-v * inv_sharp(h, 1))
    each = H // ND
    wide = lax.broadcasted_iota(jnp.int32, (R, 2 * W), 1)
    for d in range(ND):
        v = gst[d * R : (d + 1) * R]
        for n in range(each):
            v = v + jnp.where(wide == W + n, temps[d * each + n], 0.0)
        fin[d] = v
    f_begin(fin)

    def outputs(q):
        lanes = lanes_of(q)
        gl = glt[rows_of(q), :].T
        gm_ref[0, :, lanes] = bdot(gl, bt[...]).astype(bf16)
        lo_ref[0, :, lanes] = bdot(slb[:, lanes], mbs[q]).astype(bf16)
        pc_ref[0, :, lanes] = bdot(slb[:, lanes], gbs[q]).astype(bf16)

    t_onward(2)
    f_onward(1)
    for q in range(0, QN // 2):
        outputs(q)
    f_onward(2)
    for q in range(QN // 2, QN):
        outputs(q)
    gk_ref[...] = t_finish()[:, : 3 * W]
    last = f_finish()
    gs_ref[...] = last[:, :W]
    for n in range(each):
        gt_ref[n] = jnp.sum(jnp.where(wide[:1] == W + n, last[:1], 0.0))

    for h in range(H):
        f, i = h // N, h % N

        @pl.when(i != first(f))
        def _():
            phase1(h).wait_send()

    for f in range(2):
        for k in range(1, N):
            phase2(f, (second(f) + k) % N).wait_send()
            gather2(f, (second(f) + k) % N).wait_send()
            phase3(f, (first(f) + k) % N).wait_send()
    t_drain()
    f_drain()


def per_device(N, ND, node, pool, cot, w, sharp, maps):
    _, pts, width = node.shape
    H = sharp.shape[0]
    QN = H // Q
    R2 = W // N
    R = W // ND
    vmem = pl.BlockSpec(memory_space=pltpu.VMEM)
    smem = pl.BlockSpec(memory_space=pltpu.SMEM)
    hbm = pl.BlockSpec(memory_space=pltpu.HBM)
    big = jax.ShapeDtypeStruct((1, pts, width), bf16)
    dma = pltpu.SemaphoreType.DMA
    return pl.pallas_call(
        functools.partial(kernel, N, ND, H),
        out_shape=(
            big,
            big,
            big,
            jax.ShapeDtypeStruct((R, W), f32),
            jax.ShapeDtypeStruct((H // ND,), f32),
            jax.ShapeDtypeStruct((R, 3 * W), f32),
        ),
        in_specs=[hbm, hbm, hbm, vmem, smem, vmem],
        out_specs=(vmem, vmem, vmem, vmem, smem, vmem),
        scratch_shapes=[
            pltpu.VMEM((pts, width), bf16),
            pltpu.VMEM((pts, width), bf16),
            pltpu.VMEM((pts, width), bf16),
            pltpu.VMEM((width, pts), f32),
            pltpu.VMEM((width, pts), f32),
            pltpu.VMEM((width, pts), bf16),
            pltpu.VMEM((pts, width), bf16),
            pltpu.VMEM((width, pts), bf16),
            pltpu.VMEM((QW, QW), bf16),
            pltpu.VMEM((QN, QW, QW), bf16),
            pltpu.VMEM((QN, QW, QW), bf16),
            pltpu.VMEM((H, W + 8, 2 * W), f32),
            pltpu.VMEM((2, N, W + 8, 2 * W), f32),
            pltpu.VMEM((2, N, R2 + 8, 2 * W), f32),
            pltpu.VMEM((2, N, R2 + 8, 2 * W), f32),
            pltpu.VMEM((2, W, 2 * W), f32),
            pltpu.VMEM((H, W + 8, 2 * W), f32),
            pltpu.VMEM((2, W, 2 * W), f32),
            pltpu.VMEM((H, 8, pts), f32),
            pltpu.VMEM((ND, R, 4 * W), f32),
            pltpu.VMEM((ND, R, 2 * W), f32),
            pltpu.VMEM((3, max(N, ND), R, 4 * W), f32),
            pltpu.VMEM((3, max(N, ND), R, 2 * W), f32),
            dma((3, QN)),
            dma((H,)),
            dma((2, N)),
            dma((2, N)),
            dma((2, N)),
            dma((2, N)),
            dma((2, N)),
            dma((2, N)),
            dma((H,)),
            dma((3, max(N, ND))),
            dma((3, max(N, ND))),
            dma((3, max(N, ND))),
            dma((3, max(N, ND))),
        ],
        compiler_params=pltpu.CompilerParams(
            collective_id=0, has_side_effects=True, vmem_limit_bytes=32 * 1024 * 1024
        ),
    )(node, pool, cot, w, sharp, maps)


def solution(mesh):
    N = int(round(mesh.shape["point"] ** 0.5))
    ND = mesh.shape["dp"]
    big = P("dp", "point", None)
    return jax.shard_map(
        functools.partial(per_device, N, ND),
        mesh=mesh,
        in_specs=(big, big, big, P(), P(), P()),
        out_specs=(big, big, big, P("dp", None), P("dp"), P("dp", None)),
        check_vma=False,
    )
```

```python
import functools

import jax
import jax.numpy as jnp
from jax import lax
from jax.experimental import pallas as pl
from jax.experimental.pallas import tpu as pltpu
from jax.sharding import PartitionSpec as P

epsilon = 1e-05
f32 = jnp.float32
bf16 = jnp.bfloat16
W = 64
Q = 4
QW = Q * W
VMEM_LIMIT = 40 * 1024 * 1024
NN = (((1,), (0,)), ((), ()))
NT = (((1,), (1,)), ((), ()))


def bdot(a, b, dims=NN):
    return lax.dot_general(a, b, dims, preferred_element_type=f32)


def hdot(a, b, dims=NN):
    ah, bh = a.astype(bf16), b.astype(bf16)
    al, bl = (a - ah.astype(f32)).astype(bf16), (b - bh.astype(f32)).astype(bf16)
    return bdot(ah, bh, dims) + (bdot(ah, bl, dims) + bdot(al, bh, dims))


def swap_halves(x):
    return pltpu.roll(x, W, 1)


def kernel(
    N,
    ND,
    H,
    node_h,
    pool_h,
    cot_h,
    w_h,
    sharp_h,
    maps_h,
    lo_ref,
    gm_ref,
    pc_ref,
    small_ref,
    node,
    pool,
    cot,
    w_ref,
    sharp_ref,
    maps_ref,
    zed,
    sl,
    slt,
    slb,
    glt,
    gpart,
    bt,
    mbs,
    gbs,
    send1,
    recv1,
    recv2,
    res,
    acc,
    tpart,
    tgrad,
    fin,
    tred,
    fred,
    in_sem,
    par_sem,
    s1,
    r1,
    s2,
    r2,
    s3,
    r3,
    st,
    rt,
    sf,
    rf,
):
    QN = H // Q
    W2 = W // 2
    R = W // ND
    PTS = node.shape[0]
    point = lax.axis_index("point")
    me_d = lax.axis_index("dp")
    me_y = point // N
    me_z = point % N

    def first(f):
        return jnp.where(f == 0, me_y, me_z) if not isinstance(f, int) else (me_y, me_z)[f]

    def second(f):
        return jnp.where(f == 0, me_z, me_y) if not isinstance(f, int) else (me_z, me_y)[f]

    def place(f, i, j):
        if isinstance(f, int):
            return i * N + j if f == 0 else j * N + i
        return jnp.where(f == 0, i * N + j, j * N + i)

    def rcopy(src, dst, ssem, rsem, **dev):
        return pltpu.make_async_remote_copy(
            src_ref=src,
            dst_ref=dst,
            send_sem=ssem,
            recv_sem=rsem,
            device_id=dev,
            device_id_type=pl.DeviceIdType.MESH,
        )

    def wait_bytes(like, sem):
        pltpu.make_async_copy(like, like, sem).wait()

    def order(t):
        return (t % 2) * (QN // 2) + t // 2 if QN > 1 else t

    def fetch(q):
        lanes = pl.ds(pl.multiple_of(q * QW, QW), QW)
        return [
            pltpu.make_async_copy(s.at[0, :, lanes], d.at[:, lanes], in_sem.at[n, q])
            for n, (s, d) in enumerate(((node_h, node), (pool_h, pool), (cot_h, cot)))
        ]

    params = [
        pltpu.make_async_copy(s, d, par_sem.at[n])
        for n, (s, d) in enumerate(((w_h, w_ref), (sharp_h, sharp_ref), (maps_h, maps_ref)))
    ]
    for c in params:
        c.start()
    for t in range(QN):
        for c in fetch(order(t)):
            c.start()

    barrier = pltpu.get_barrier_semaphore()
    for k in range(1, N):
        for dev in (place(0, (me_y + k) % N, me_z), place(0, me_y, (me_z + k) % N)):
            pl.semaphore_signal(
                barrier, inc=1, device_id={"point": dev}, device_id_type=pl.DeviceIdType.MESH
            )
    for k in range(1, ND):
        pl.semaphore_signal(
            barrier,
            inc=1,
            device_id={"dp": (me_d + k) % ND},
            device_id_type=pl.DeviceIdType.MESH,
        )

    for c in params:
        c.wait()
    w4 = jnp.concatenate([w_ref[...].astype(f32)] * Q, axis=0)
    w4 = jnp.concatenate([w4] * Q, axis=1)
    row = lax.broadcasted_iota(jnp.int32, (QW, QW), 0)
    col = lax.broadcasted_iota(jnp.int32, (QW, QW), 1)
    w4 = jnp.where(row // W == col // W, w4, 0.0)
    bt[...] = w4.T.astype(bf16)
    low = lax.broadcasted_iota(jnp.int32, (W, 2 * W), 1) < W
    low2 = low[:W2]

    def inv_sharp(h, width):
        return 1.0 / jnp.full((1, width), sharp_ref[h], f32)

    def rows_of(q, i=0, n=QW):
        return pl.ds(pl.multiple_of(q * QW + i * W, W), n)

    def lanes_of(q):
        return pl.ds(pl.multiple_of(q * QW, QW), QW)

    def fold(x, i):
        if i % 2 == 0:
            return jnp.where(low2, x[:W2], swap_halves(x[W2:]))
        return jnp.where(low2, swap_halves(x[:W2]), x[W2:])

    def unfold(x):
        return jnp.concatenate([x[:, :W], swap_halves(x)[:, :W]], axis=0)

    def spread(x, i):
        other = swap_halves(x)
        up, down = (x, other) if i % 2 == 0 else (other, x)
        keep = low2 if i % 2 == 0 else ~low2
        return jnp.concatenate([jnp.where(keep, up, 0.0), jnp.where(keep, down, 0.0)], axis=0)

    def column(row):
        return jnp.broadcast_to(row, (8, 2 * W)).T[:, :1]

    rows_in = (W2 + 1, W2)
    rows_out = (W2, W2 + 1)

    def phase1(s, h, f, i):
        n = pl.ds(0, rows_in[s])
        return rcopy(
            send1.at[s, h, n],
            recv1.at[s, f, first(f), n],
            s1.at[s],
            r1.at[s, f],
            point=place(f, i, second(f)),
        )

    def forward(t, carry):
        q = order(t)
        for c in fetch(q):
            c.wait()
        z = bdot(bt[...], node[:, lanes_of(q)], NT)
        sums = []
        for i in range(Q):
            zh = z[i * W : (i + 1) * W] * inv_sharp(q * Q + i, PTS)
            e = jnp.exp(zh - jnp.max(zh, axis=0, keepdims=True))
            s = e * (1.0 / jnp.sum(e, axis=0, keepdims=True))
            sb = s.astype(bf16)
            zed[rows_of(q, i, W), :] = zh
            sl[rows_of(q, i, W), :] = s
            slt[rows_of(q, i, W), :] = sb
            sums.append(sum(s[:, c : c + 2 * W] for c in range(0, PTS, 2 * W)))
        sq = slt[rows_of(q), :]
        sums = jnp.concatenate(sums, axis=0)
        top = sums.astype(bf16)
        ones = jnp.ones((8, 2 * W), bf16)
        mass = bdot(ones, top, NT) + bdot(ones, (sums - top.astype(f32)).astype(bf16), NT)
        pooled = bdot(sq, pool[:, lanes_of(q)])
        gmixed = bdot(sq, cot[:, lanes_of(q)])
        for i in range(Q):
            r, c = slice(i * W, (i + 1) * W), slice(i // 2 * 2 * W, (i // 2 + 1) * 2 * W)
            m = mass[:, c] if i % 2 == 0 else swap_halves(mass[:, c])
            send1[0, q * Q + i, :W2, :] = fold(pooled[r, c], i)
            send1[0, q * Q + i, W2:, :] = m
            send1[1, q * Q + i, :W2, :] = fold(gmixed[r, c], i)

        @pl.when(t == 0)
        def _():
            pl.semaphore_wait(barrier, 2 * (N - 1) + ND - 1)

        for s in range(2):
            for i in range(Q):
                h = q * Q + i

                @pl.when(h % N != first(h // N))
                def _():
                    phase1(s, h, h // N, h % N).start()

        return carry

    lax.fori_loop(0, QN, forward, 0)

    def flip(q):
        slb[:, lanes_of(q)] = slt[rows_of(q), :].T

    for q in range(QN):
        flip(q)

    def phase2(s, f, j):
        mine = recv2.at[s, f, second(f), pl.ds(0, rows_in[s])]
        return rcopy(
            mine, mine, s2.at[s], r2.at[s, f], point=place(f, first(f), j)
        )

    def arrived1(s, f):
        h = f * N + first(f)
        own = send1[s, h]
        recv1[s, f, first(f)] = own
        wait_bytes(recv1.at[s, f, pl.ds(0, N - 1), pl.ds(0, rows_in[s])], r1.at[s, f])
        n = rows_in[s]
        part = recv1[s, f, 0, :n, :]
        for i in range(1, N):
            part = part + recv1[s, f, i, :n, :]
        recv2[s, f, second(f), :n, :] = part
        for k in range(1, N):
            phase2(s, f, (second(f) + k) % N).start()

    def arrived2(s, f):
        n = rows_in[s]
        wait_bytes(recv2.at[s, f, pl.ds(0, N - 1), pl.ds(0, n)], r2.at[s, f])
        total = recv2[s, f, 0, :n, :]
        for j in range(1, N):
            total = total + recv2[s, f, j, :n, :]
        return total

    for s in range(2):
        for f in range(2):
            arrived1(s, f)

    for q in range(QN):
        mbs[q] = jnp.zeros((QW, QW), bf16)
        gbs[q] = jnp.zeros((QW, QW), bf16)
    acc[...] = jnp.zeros(acc.shape, f32)

    maps = maps_ref[...]

    def phase3(s, f, i):
        h = f * N + first(f)
        mine = res.at[s, h, pl.ds(0, rows_out[s])]
        return rcopy(
            mine, mine, s3.at[s], r3.at[s, f], point=place(f, i, second(f))
        )

    def send3(s, f):
        for k in range(1, N):
            phase3(s, f, (first(f) + k) % N).start()

    totals = [arrived2(0, f) for f in range(2)]
    mass = jnp.concatenate([total[W2:] for total in totals], axis=0)
    mass = jnp.concatenate([mass, jnp.ones((6, 2 * W), f32)], axis=0).T
    inverse = 1.0 / (jnp.concatenate([mass[:W, :1], mass[:W, 1:2]], axis=0) + epsilon)
    t = jnp.concatenate([unfold(total[:W2]) for total in totals], axis=0) * inverse
    proj = hdot(t, maps)
    query, key, value = proj[:, :W], swap_halves(proj[:, : 2 * W])[:, :W], proj[:, 2 * W :]
    score = hdot(query, key, NT) * W**-0.5
    row = lax.broadcasted_iota(jnp.int32, (2 * W, 2 * W), 0)
    col = lax.broadcasted_iota(jnp.int32, (2 * W, 2 * W), 1)
    score = jnp.where(row // W == col // W, score, -jnp.inf)
    e = jnp.exp(score - jnp.max(score, axis=1, keepdims=True))
    attn = e / jnp.sum(e, axis=1, keepdims=True)
    mixed = hdot(attn, value).astype(bf16).astype(f32)
    for f in range(2):
        res[0, f * N + first(f), :W2, :] = jnp.concatenate(
            [mixed[f * W : f * W + W2], mixed[f * W + W2 : (f + 1) * W]], axis=1
        )
        send3(0, f)

    gmix = jnp.concatenate([unfold(arrived2(1, f)) for f in range(2)], axis=0)
    gattn = hdot(gmix, value, NT)
    gvalue = hdot(attn.T, gmix)
    gscore = attn * (gattn - jnp.sum(attn * gattn, axis=1, keepdims=True)) * W**-0.5
    gquery = hdot(gscore, key)
    gkey = hdot(gscore.T, query)
    gproj = jnp.concatenate([gquery, gkey, gvalue], axis=1)
    gtok = hdot(gproj, maps, NT)
    gpool = (gtok * inverse).astype(bf16).astype(f32)
    gmass = hdot(jnp.ones((8, W), f32), -(gtok * t) * inverse, NT)
    for f in range(2):
        h = f * N + first(f)
        res[1, h, :W2, :] = jnp.concatenate(
            [gpool[f * W : f * W + W2], gpool[f * W + W2 : (f + 1) * W]], axis=1
        )
        here, there = (gmass, swap_halves(gmass)) if f == 0 else (swap_halves(gmass), gmass)
        even = (jnp.zeros((8, 2 * W), jnp.int32) + h) % 2 == 0
        res[1, h, W2:, :] = jnp.where(
            even, jnp.where(low[:8], here, 0.0), jnp.where(low[:8], 0.0, there)
        )
        send3(1, f)

    def all_of(buf, ssem, rsem):
        axes = ((me_d, ND), (me_z, N), (me_y, N))

        def dev(stage, k):
            if stage == 0:
                return {"dp": k}
            return {"point": place(0, me_y, k) if stage == 1 else place(0, k, me_z)}

        def copy(stage, k, src):
            me = axes[stage][0]
            return rcopy(
                src, buf.at[stage, me], ssem.at[stage], rsem.at[stage], **dev(stage, k)
            )

        def send(stage, source):
            me, n = axes[stage]
            for k in range(1, n):
                k = (me + k) % n
                copy(stage, k, source(k)).start()

        def receive(stage):
            me, n = axes[stage]
            wait_bytes(buf.at[stage, pl.ds(0, n - 1)], rsem.at[stage])
            total = buf[stage, 0]
            for k in range(1, n):
                total = total + buf[stage, k]
            return total

        def begin(source):
            buf[0, me_d] = source[me_d]
            send(0, lambda k: source.at[k])

        def onward(stage):
            total = receive(stage - 1)
            me = axes[stage][0]
            buf[stage, me] = total
            send(stage, lambda k: buf.at[stage, me])

        def finish():
            return receive(2)

        def drain():
            for stage in range(3):
                n = axes[stage][1]
                wait_bytes(buf.at[stage, pl.ds(0, n - 1)], ssem.at[stage])

        return begin, onward, finish, drain

    t_begin, t_onward, t_finish, t_drain = all_of(tred, st, rt)
    f_begin, f_onward, f_finish, f_drain = all_of(fred, sf, rf)

    tg = hdot(t.T, gproj) * (1.0 / N)
    tg = jnp.concatenate([tg, jnp.zeros((W, W), f32)], axis=1)
    for d in range(ND):
        tgrad[d] = tg[d * R : (d + 1) * R]
    t_begin(tgrad)

    def halves(s, body):
        for f in range(2):
            wait_bytes(res.at[s, pl.ds(0, N - 1), pl.ds(0, rows_out[s])], r3.at[s, f])
            if QN > 1:
                lax.fori_loop(f * (QN // 2), (f + 1) * (QN // 2), body, 0)
        if QN == 1:
            body(0, 0)

    def pair(i):
        return slice(i // 2 * 2 * W, (i // 2 + 1) * 2 * W)

    def with_mixed(q, carry):
        for i in range(Q):
            mbs[q, i * W : (i + 1) * W, pair(i)] = spread(res[0, q * Q + i, :W2, :], i).astype(bf16)
        gpart[rows_of(q), :] = bdot(mbs[q], cot[:, lanes_of(q)], NT)
        lo_ref[0, :, lanes_of(q)] = bdot(slb[:, lanes_of(q)], mbs[q]).astype(bf16)
        return carry

    halves(0, with_mixed)
    t_onward(1)

    def backward(q, carry):
        cols = []
        for i in range(Q):
            gbs[q, i * W : (i + 1) * W, pair(i)] = spread(res[1, q * Q + i, :W2, :], i).astype(bf16)
            if i % 2 == 0:
                cols.append(
                    column(
                        res[1, q * Q + i, W2 : W2 + 1, :] + res[1, q * Q + i + 1, W2 : W2 + 1, :]
                    )
                )
        gq = gpart[rows_of(q), :] + bdot(gbs[q], pool[:, lanes_of(q)], NT)
        for i in range(Q):
            h = q * Q + i
            s = sl[rows_of(q, i, W), :]
            g = gq[i * W : (i + 1) * W] + cols[i // 2][i % 2 * W : (i % 2 + 1) * W]
            sg = s * g
            gz = sg - s * jnp.sum(sg, axis=0, keepdims=True)
            glt[rows_of(q, i, W), :] = (gz * inv_sharp(h, PTS)).astype(bf16)
            tz = gz * zed[rows_of(q, i, W), :]
            tpart[h] = jnp.sum(tz.reshape(W // 8, 8, PTS), axis=0)
        gs = bdot(glt[rows_of(q), :], node[:, lanes_of(q)])
        for i in range(Q):
            acc[i % 2] += gs[i * W : (i + 1) * W, pair(i)]
        return carry

    halves(1, backward)

    gst = jnp.where(low, acc[0] + swap_halves(acc[1]), 0.0)
    gst = jnp.concatenate([gst, jnp.zeros((W, 2 * W), f32)], axis=0).T[:W]
    temps = []
    for h in range(H):
        v = jnp.sum(jnp.sum(tpart[h], axis=0, keepdims=True), axis=1, keepdims=True)
        temps.append(-v * inv_sharp(h, 1))
    each = H // ND
    wide = lax.broadcasted_iota(jnp.int32, (R, 2 * W), 1)
    for d in range(ND):
        v = gst[d * R : (d + 1) * R]
        for n in range(each):
            v = v + jnp.where(wide == W + n, temps[d * each + n], 0.0)
        fin[d] = v
    f_begin(fin)

    def outputs(q):
        gl = glt[rows_of(q), :].T
        gm_ref[0, :, lanes_of(q)] = bdot(gl, bt[...]).astype(bf16)
        pc_ref[0, :, lanes_of(q)] = bdot(slb[:, lanes_of(q)], gbs[q]).astype(bf16)

    t_onward(2)
    for q in range(QN):
        outputs(q)
    f_onward(1)
    for s in range(2):
        wait_bytes(send1.at[s, pl.ds(0, 2 * N - 2), pl.ds(0, rows_in[s])], s1.at[s])
        wait_bytes(recv2.at[s, :, pl.ds(0, N - 1), pl.ds(0, rows_in[s])], s2.at[s])
        wait_bytes(res.at[s, pl.ds(0, 2 * N - 2), pl.ds(0, rows_out[s])], s3.at[s])
    f_onward(2)
    small_ref[:, 2 * W :] = t_finish()
    t_drain()
    small_ref[:, : 2 * W] = f_finish()
    f_drain()


def finish_kernel(
    each,
    lo_i,
    gm_i,
    pc_i,
    small,
    lo_h,
    gm_h,
    pc_h,
    gs_h,
    gt_h,
    gk_h,
    gs,
    gk,
    gt,
    sem,
):
    pairs = [(lo_i, lo_h), (gm_i, gm_h), (pc_i, pc_h), (gs, gs_h), (gk, gk_h), (gt, gt_h)]
    copies = [pltpu.make_async_copy(s, d, sem.at[n]) for n, (s, d) in enumerate(pairs)]
    for c in copies[:3]:
        c.start()
    gs[...] = small[:, :W]
    gk[...] = small[:, 2 * W : 5 * W]
    spot = lax.broadcasted_iota(jnp.int32, (1, 2 * W), 1)
    for n in range(each):
        gt[n] = jnp.sum(jnp.where(spot == W + n, small[:1, : 2 * W], 0.0))
    for c in copies[3:]:
        c.start()
    for c in copies:
        c.wait()


def per_device(N, ND, node, pool, cot, w, sharp, maps):
    _, pts, width = node.shape
    H = sharp.shape[0]
    QN = H // Q
    W2 = W // 2
    R = W // ND
    any_ = pl.BlockSpec(memory_space=pl.ANY)
    vmem = pl.BlockSpec(memory_space=pltpu.VMEM)
    big = jax.ShapeDtypeStruct((1, pts, width), bf16)
    dma = pltpu.SemaphoreType.DMA
    node, pool, cot, w, sharp, maps = (
        pltpu.with_memory_space_constraint(a, pltpu.HBM) for a in (node, pool, cot, w, sharp, maps)
    )
    lo, gm, pc, small = pl.pallas_call(
        functools.partial(kernel, N, ND, H),
        out_shape=(big, big, big, jax.ShapeDtypeStruct((R, 6 * W), f32)),
        in_specs=[any_] * 6,
        out_specs=[vmem] * 4,
        scratch_shapes=[
            pltpu.VMEM((pts, width), bf16),
            pltpu.VMEM((pts, width), bf16),
            pltpu.VMEM((pts, width), bf16),
            pltpu.VMEM((W, W), bf16),
            pltpu.SMEM((H,), f32),
            pltpu.VMEM((W, 3 * W), f32),
            pltpu.VMEM((width, pts), f32),
            pltpu.VMEM((width, pts), f32),
            pltpu.VMEM((width, pts), bf16),
            pltpu.VMEM((pts, width), bf16),
            pltpu.VMEM((width, pts), bf16),
            pltpu.VMEM((width, pts), f32),
            pltpu.VMEM((QW, QW), bf16),
            pltpu.VMEM((QN, QW, QW), bf16),
            pltpu.VMEM((QN, QW, QW), bf16),
            pltpu.VMEM((2, H, W2 + 8, 2 * W), f32),
            pltpu.VMEM((2, 2, N, W2 + 8, 2 * W), f32),
            pltpu.VMEM((2, 2, N, W2 + 8, 2 * W), f32),
            pltpu.VMEM((2, H, W2 + 8, 2 * W), f32),
            pltpu.VMEM((2, W, 2 * W), f32),
            pltpu.VMEM((H, 8, pts), f32),
            pltpu.VMEM((ND, R, 4 * W), f32),
            pltpu.VMEM((ND, R, 2 * W), f32),
            pltpu.VMEM((3, max(N, ND), R, 4 * W), f32),
            pltpu.VMEM((3, max(N, ND), R, 2 * W), f32),
            dma((3, QN)),
            dma((3,)),
            dma((2,)),
            dma((2, 2)),
            dma((2,)),
            dma((2, 2)),
            dma((2,)),
            dma((2, 2)),
            dma((3,)),
            dma((3,)),
            dma((3,)),
            dma((3,)),
        ],
        compiler_params=pltpu.CompilerParams(
            collective_id=0, has_side_effects=True, vmem_limit_bytes=VMEM_LIMIT
        ),
    )(node, pool, cot, w, sharp, maps)
    each = H // ND
    return pl.pallas_call(
        functools.partial(finish_kernel, each),
        out_shape=(
            big,
            big,
            big,
            jax.ShapeDtypeStruct((R, W), f32),
            jax.ShapeDtypeStruct((each,), f32),
            jax.ShapeDtypeStruct((R, 3 * W), f32),
        ),
        in_specs=[vmem] * 4,
        out_specs=[any_] * 6,
        scratch_shapes=[
            pltpu.VMEM((R, W), f32),
            pltpu.VMEM((R, 3 * W), f32),
            pltpu.SMEM((each,), f32),
            dma((6,)),
        ],
        compiler_params=pltpu.CompilerParams(vmem_limit_bytes=VMEM_LIMIT),
    )(lo, gm, pc, small)


def solution(mesh):
    N = int(round(mesh.shape["point"] ** 0.5))
    ND = mesh.shape["dp"]
    big = P("dp", "point", None)
    return jax.shard_map(
        functools.partial(per_device, N, ND),
        mesh=mesh,
        in_specs=(big, big, big, P(), P(), P()),
        out_specs=(big, big, big, P("dp", None), P("dp"), P("dp", None)),
        check_vma=False,
    )
```

```python
import functools

import jax
import jax.numpy as jnp
from jax import lax
from jax.experimental import pallas as pl
from jax.experimental.pallas import tpu as pltpu
from jax.sharding import PartitionSpec as P

epsilon = 1e-05
f32 = jnp.float32
bf16 = jnp.bfloat16
W = 64
Q = 4
QW = Q * W
BANDS = 1
VMEM_LIMIT = 40 * 1024 * 1024
NN = (((1,), (0,)), ((), ()))
NT = (((1,), (1,)), ((), ()))


def bdot(a, b, dims=NN):
    return lax.dot_general(a, b, dims, preferred_element_type=f32)


def hdot(a, b, dims=NN):
    ah, bh = a.astype(bf16), b.astype(bf16)
    al, bl = (a - ah.astype(f32)).astype(bf16), (b - bh.astype(f32)).astype(bf16)
    return bdot(ah, bh, dims) + (bdot(ah, bl, dims) + bdot(al, bh, dims))


def swap_halves(x):
    return pltpu.roll(x, W, 1)


def kernel(
    N,
    ND,
    H,
    node_h,
    pool_h,
    cot_h,
    w_h,
    sharp_h,
    maps_h,
    lo_ref,
    gm_ref,
    pc_ref,
    small_ref,
    node,
    pool,
    cot,
    w_ref,
    sharp_ref,
    maps_ref,
    zed,
    sl,
    slt,
    slb,
    glt,
    gpart,
    bt,
    mbs,
    gbs,
    send1,
    recv1,
    recv2,
    res,
    acc,
    tpart,
    tgrad,
    fin,
    tred,
    fred,
    in_sem,
    par_sem,
    s1,
    r1,
    s2,
    r2,
    s3,
    r3,
    st,
    rt,
    sf,
    rf,
):
    QN = H // Q
    W2 = W // 2
    R = W // ND
    PTS = node.shape[0]
    point = lax.axis_index("point")
    me_d = lax.axis_index("dp")
    me_y = point // N
    me_z = point % N

    def first(f):
        return jnp.where(f == 0, me_y, me_z) if not isinstance(f, int) else (me_y, me_z)[f]

    def second(f):
        return jnp.where(f == 0, me_z, me_y) if not isinstance(f, int) else (me_z, me_y)[f]

    def place(f, i, j):
        if isinstance(f, int):
            return i * N + j if f == 0 else j * N + i
        return jnp.where(f == 0, i * N + j, j * N + i)

    def far_first(n):
        return sorted(range(1, n), key=lambda k: -min(k, n - k))

    def rcopy(src, dst, ssem, rsem, **dev):
        return pltpu.make_async_remote_copy(
            src_ref=src,
            dst_ref=dst,
            send_sem=ssem,
            recv_sem=rsem,
            device_id=dev,
            device_id_type=pl.DeviceIdType.MESH,
        )

    def wait_bytes(like, sem):
        pltpu.make_async_copy(like, like, sem).wait()

    def order(t):
        return (t % 2) * (QN // 2) + t // 2 if QN > 1 else t

    def fetch(q):
        lanes = pl.ds(pl.multiple_of(q * QW, QW), QW)
        return [
            pltpu.make_async_copy(s.at[0, :, lanes], d.at[:, lanes], in_sem.at[n, q])
            for n, (s, d) in enumerate(((node_h, node), (pool_h, pool), (cot_h, cot)))
        ]

    params = [
        pltpu.make_async_copy(s, d, par_sem.at[n])
        for n, (s, d) in enumerate(((w_h, w_ref), (sharp_h, sharp_ref), (maps_h, maps_ref)))
    ]
    for c in params:
        c.start()
    for t in range(QN):
        for c in fetch(order(t)):
            c.start()

    barrier = pltpu.get_barrier_semaphore()
    for k in range(1, N):
        for dev in (place(0, (me_y + k) % N, me_z), place(0, me_y, (me_z + k) % N)):
            pl.semaphore_signal(
                barrier, inc=1, device_id={"point": dev}, device_id_type=pl.DeviceIdType.MESH
            )
    for k in range(1, ND):
        pl.semaphore_signal(
            barrier,
            inc=1,
            device_id={"dp": (me_d + k) % ND},
            device_id_type=pl.DeviceIdType.MESH,
        )

    for c in params:
        c.wait()
    w4 = jnp.concatenate([w_ref[...].astype(f32)] * Q, axis=0)
    w4 = jnp.concatenate([w4] * Q, axis=1)
    row = lax.broadcasted_iota(jnp.int32, (QW, QW), 0)
    col = lax.broadcasted_iota(jnp.int32, (QW, QW), 1)
    w4 = jnp.where(row // W == col // W, w4, 0.0)
    bt[...] = w4.T.astype(bf16)
    low = lax.broadcasted_iota(jnp.int32, (W, 2 * W), 1) < W
    low2 = low[:W2]

    def inv_sharp(h, width):
        return 1.0 / jnp.full((1, width), sharp_ref[h], f32)

    def rows_of(q, i=0, n=QW):
        return pl.ds(pl.multiple_of(q * QW + i * W, W), n)

    def lanes_of(q):
        return pl.ds(pl.multiple_of(q * QW, QW), QW)

    def fold(x, i):
        if i % 2 == 0:
            return jnp.where(low2, x[:W2], swap_halves(x[W2:]))
        return jnp.where(low2, swap_halves(x[:W2]), x[W2:])

    def unfold(x):
        return jnp.concatenate([x[:, :W], swap_halves(x)[:, :W]], axis=0)

    def spread(x, i):
        other = swap_halves(x)
        up, down = (x, other) if i % 2 == 0 else (other, x)
        keep = low2 if i % 2 == 0 else ~low2
        return jnp.concatenate([jnp.where(keep, up, 0.0), jnp.where(keep, down, 0.0)], axis=0)

    def column(row):
        return jnp.broadcast_to(row, (8, 2 * W)).T[:, :1]

    rows_in = (W2 + 1, W2)
    rows_out = (W2, W2 + 1)

    def phase1(s, h, f, i):
        n = pl.ds(0, rows_in[s])
        return rcopy(
            send1.at[s, h, n],
            recv1.at[s, f, first(f), n],
            s1.at[s],
            r1.at[s, f],
            point=place(f, i, second(f)),
        )

    def forward(t):
        q = order(t)
        for c in fetch(q):
            c.wait()
        z = bdot(bt[...], node[:, lanes_of(q)], NT)
        sums = []
        for i in range(Q):
            zh = z[i * W : (i + 1) * W] * inv_sharp(q * Q + i, PTS)
            e = jnp.exp(zh - jnp.max(zh, axis=0, keepdims=True))
            s = e * (1.0 / jnp.sum(e, axis=0, keepdims=True))
            sb = s.astype(bf16)
            zed[rows_of(q, i, W), :] = zh
            sl[rows_of(q, i, W), :] = s
            slt[rows_of(q, i, W), :] = sb
            sums.append(sum(s[:, c : c + 2 * W] for c in range(0, PTS, 2 * W)))
        sq = slt[rows_of(q), :]
        sums = jnp.concatenate(sums, axis=0)
        top = sums.astype(bf16)
        ones = jnp.ones((8, 2 * W), bf16)
        mass = bdot(ones, top, NT) + bdot(ones, (sums - top.astype(f32)).astype(bf16), NT)
        pooled = bdot(sq, pool[:, lanes_of(q)])
        gmixed = bdot(sq, cot[:, lanes_of(q)])
        for i in range(Q):
            r, c = slice(i * W, (i + 1) * W), slice(i // 2 * 2 * W, (i // 2 + 1) * 2 * W)
            m = mass[:, c] if i % 2 == 0 else swap_halves(mass[:, c])
            send1[0, q * Q + i, :W2, :] = fold(pooled[r, c], i)
            send1[0, q * Q + i, W2:, :] = m
            send1[1, q * Q + i, :W2, :] = fold(gmixed[r, c], i)

        if t == 0:
            pl.semaphore_wait(barrier, 2 * (N - 1) + ND - 1)

        for s in range(2):
            for i in range(Q):
                h = q * Q + i

                @pl.when(h % N != first(h // N))
                def _():
                    phase1(s, h, h // N, h % N).start()

    for t in range(QN):
        forward(t)

    def flip(q):
        slb[:, lanes_of(q)] = slt[rows_of(q), :].T

    for q in range(QN):
        flip(q)

    def phase2(s, f, j):
        mine = recv2.at[s, f, second(f), pl.ds(0, rows_in[s])]
        return rcopy(
            mine, mine, s2.at[s], r2.at[s, f], point=place(f, first(f), j)
        )

    def arrived1(s, f):
        h = f * N + first(f)
        own = send1[s, h]
        recv1[s, f, first(f)] = own
        wait_bytes(recv1.at[s, f, pl.ds(0, N - 1), pl.ds(0, rows_in[s])], r1.at[s, f])
        n = rows_in[s]
        part = recv1[s, f, 0, :n, :]
        for i in range(1, N):
            part = part + recv1[s, f, i, :n, :]
        recv2[s, f, second(f), :n, :] = part
        for k in far_first(N):
            phase2(s, f, (second(f) + k) % N).start()

    def arrived2(s, f):
        n = rows_in[s]
        wait_bytes(recv2.at[s, f, pl.ds(0, N - 1), pl.ds(0, n)], r2.at[s, f])
        total = recv2[s, f, 0, :n, :]
        for j in range(1, N):
            total = total + recv2[s, f, j, :n, :]
        return total

    for s in range(2):
        for f in range(2):
            arrived1(s, f)

    for q in range(QN):
        mbs[q] = jnp.zeros((QW, QW), bf16)
        gbs[q] = jnp.zeros((QW, QW), bf16)
    acc[...] = jnp.zeros(acc.shape, f32)

    maps = maps_ref[...]

    def phase3(s, f, i):
        h = f * N + first(f)
        mine = res.at[s, h, pl.ds(0, rows_out[s])]
        return rcopy(
            mine, mine, s3.at[s], r3.at[s, f], point=place(f, i, second(f))
        )

    def send3(s, f):
        for k in far_first(N):
            phase3(s, f, (first(f) + k) % N).start()

    totals = [arrived2(0, f) for f in range(2)]
    mass = jnp.concatenate([total[W2:] for total in totals], axis=0)
    mass = jnp.concatenate([mass, jnp.ones((6, 2 * W), f32)], axis=0).T
    inverse = 1.0 / (jnp.concatenate([mass[:W, :1], mass[:W, 1:2]], axis=0) + epsilon)
    t = jnp.concatenate([unfold(total[:W2]) for total in totals], axis=0) * inverse
    proj = hdot(t, maps)
    query, key, value = proj[:, :W], swap_halves(proj[:, : 2 * W])[:, :W], proj[:, 2 * W :]
    score = hdot(query, key, NT) * W**-0.5
    row = lax.broadcasted_iota(jnp.int32, (2 * W, 2 * W), 0)
    col = lax.broadcasted_iota(jnp.int32, (2 * W, 2 * W), 1)
    score = jnp.where(row // W == col // W, score, -jnp.inf)
    e = jnp.exp(score - jnp.max(score, axis=1, keepdims=True))
    attn = e / jnp.sum(e, axis=1, keepdims=True)
    mixed = hdot(attn, value).astype(bf16).astype(f32)
    for f in range(2):
        res[0, f * N + first(f), :W2, :] = jnp.concatenate(
            [mixed[f * W : f * W + W2], mixed[f * W + W2 : (f + 1) * W]], axis=1
        )
        send3(0, f)

    gmix = jnp.concatenate([unfold(arrived2(1, f)) for f in range(2)], axis=0)
    gattn = hdot(gmix, value, NT)
    gvalue = hdot(attn.T, gmix)
    gscore = attn * (gattn - jnp.sum(attn * gattn, axis=1, keepdims=True)) * W**-0.5
    gquery = hdot(gscore, key)
    gkey = hdot(gscore.T, query)
    gproj = jnp.concatenate([gquery, gkey, gvalue], axis=1)
    gtok = hdot(gproj, maps, NT)
    gpool = (gtok * inverse).astype(bf16).astype(f32)
    gmass = hdot(jnp.ones((8, W), f32), -(gtok * t) * inverse, NT)
    for f in range(2):
        h = f * N + first(f)
        res[1, h, :W2, :] = jnp.concatenate(
            [gpool[f * W : f * W + W2], gpool[f * W + W2 : (f + 1) * W]], axis=1
        )
        here, there = (gmass, swap_halves(gmass)) if f == 0 else (swap_halves(gmass), gmass)
        even = (jnp.zeros((8, 2 * W), jnp.int32) + h) % 2 == 0
        res[1, h, W2:, :] = jnp.where(
            even, jnp.where(low[:8], here, 0.0), jnp.where(low[:8], 0.0, there)
        )
        send3(1, f)

    def all_of(buf, ssem, rsem):
        axes = ((me_d, ND), (me_z, N), (me_y, N))

        def dev(stage, k):
            if stage == 0:
                return {"dp": k}
            return {"point": place(0, me_y, k) if stage == 1 else place(0, k, me_z)}

        def copy(stage, k, src):
            me = axes[stage][0]
            return rcopy(
                src, buf.at[stage, me], ssem.at[stage], rsem.at[stage], **dev(stage, k)
            )

        def send(stage, source):
            me, n = axes[stage]
            for k in far_first(n):
                k = (me + k) % n
                copy(stage, k, source(k)).start()

        def receive(stage):
            me, n = axes[stage]
            wait_bytes(buf.at[stage, pl.ds(0, n - 1)], rsem.at[stage])
            total = buf[stage, 0]
            for k in range(1, n):
                total = total + buf[stage, k]
            return total

        def begin(source):
            buf[0, me_d] = source[me_d]
            send(0, lambda k: source.at[k])

        def onward(stage):
            total = receive(stage - 1)
            me = axes[stage][0]
            buf[stage, me] = total
            send(stage, lambda k: buf.at[stage, me])

        def finish():
            return receive(2)

        def drain():
            for stage in range(3):
                n = axes[stage][1]
                wait_bytes(buf.at[stage, pl.ds(0, n - 1)], ssem.at[stage])

        return begin, onward, finish, drain

    t_begin, t_onward, t_finish, t_drain = all_of(tred, st, rt)
    f_begin, f_onward, f_finish, f_drain = all_of(fred, sf, rf)

    tg = hdot(t.T, gproj) * (1.0 / N)
    tg = jnp.concatenate([tg, jnp.zeros((W, W), f32)], axis=1)
    for d in range(ND):
        tgrad[d] = tg[d * R : (d + 1) * R]
    t_begin(tgrad)

    def halves(s, body):
        for f in range(2):
            wait_bytes(res.at[s, pl.ds(0, N - 1), pl.ds(0, rows_out[s])], r3.at[s, f])
            if QN > 1:
                for q in range(f * (QN // 2), (f + 1) * (QN // 2)):
                    body(q)
        if QN == 1:
            body(0)

    def pair(i):
        return slice(i // 2 * 2 * W, (i // 2 + 1) * 2 * W)

    def with_mixed(q):
        for i in range(Q):
            mbs[q, i * W : (i + 1) * W, pair(i)] = spread(res[0, q * Q + i, :W2, :], i).astype(bf16)
        gpart[rows_of(q), :] = bdot(mbs[q], cot[:, lanes_of(q)], NT)
        lo_ref[0, :, lanes_of(q)] = bdot(slb[:, lanes_of(q)], mbs[q]).astype(bf16)

    halves(0, with_mixed)
    t_onward(1)

    quarter = lax.broadcasted_iota(jnp.int32, (8, 2 * W), 1) // W2

    def backward(q):
        cols = []
        for i in range(Q):
            gbs[q, i * W : (i + 1) * W, pair(i)] = spread(res[1, q * Q + i, :W2, :], i).astype(bf16)
            if i % 2 == 0:
                cols.append(
                    column(
                        res[1, q * Q + i, W2 : W2 + 1, :] + res[1, q * Q + i + 1, W2 : W2 + 1, :]
                    )
                )
        part = None
        gq = gpart[rows_of(q), :] + bdot(gbs[q], pool[:, lanes_of(q)], NT)
        for i in range(Q):
            h = q * Q + i
            s = sl[rows_of(q, i, W), :]
            g = gq[i * W : (i + 1) * W] + cols[i // 2][i % 2 * W : (i % 2 + 1) * W]
            sg = s * g
            gz = sg - s * jnp.sum(sg, axis=0, keepdims=True)
            glt[rows_of(q, i, W), :] = (gz * inv_sharp(h, PTS)).astype(bf16)
            tz = gz * zed[rows_of(q, i, W), :]
            tz = jnp.sum(tz.reshape(W // 8, 8, PTS), axis=0)
            tz = sum(tz[:, c : c + 2 * W] for c in range(0, PTS, 2 * W))
            tz = tz + swap_halves(tz)
            tz = (tz + pltpu.roll(tz, W2, 1)) * inv_sharp(h, 2 * W)
            part = jnp.where(quarter == 2 + i % 2, -tz, part if i % 2 else 0.0)
            if i % 2:
                tpart[h // 2] = part
        gs = bdot(glt[rows_of(q), :], node[:, lanes_of(q)])
        for i in range(Q):
            acc[i % 2] += gs[i * W : (i + 1) * W, pair(i)]

    halves(1, backward)

    gst = jnp.where(low, acc[0] + swap_halves(acc[1]), 0.0)
    gst = jnp.concatenate([gst, jnp.zeros((W, 2 * W), f32)], axis=0).T[:W]
    for d in range(ND):
        fin[d] = gst[d * R : (d + 1) * R]
        fin[d, :8, :] = fin[d, :8, :] + tpart[d]
    f_begin(fin)

    def outputs(q):
        gl = glt[rows_of(q), :].T
        gm_ref[0, :, lanes_of(q)] = bdot(gl, bt[...]).astype(bf16)
        pc_ref[0, :, lanes_of(q)] = bdot(slb[:, lanes_of(q)], gbs[q]).astype(bf16)

    t_onward(2)
    for q in range(QN):
        outputs(q)
    f_onward(1)
    for s in range(2):
        wait_bytes(send1.at[s, pl.ds(0, 2 * N - 2), pl.ds(0, rows_in[s])], s1.at[s])
        wait_bytes(recv2.at[s, :, pl.ds(0, N - 1), pl.ds(0, rows_in[s])], s2.at[s])
        wait_bytes(res.at[s, pl.ds(0, 2 * N - 2), pl.ds(0, rows_out[s])], s3.at[s])
    f_onward(2)
    small_ref[:, 2 * W :] = t_finish()
    t_drain()
    small_ref[:, : 2 * W] = f_finish()
    f_drain()


def finish_kernel(
    lo_i,
    gm_i,
    pc_i,
    small,
    lo_h,
    gm_h,
    pc_h,
    gs_h,
    gt_h,
    gk_h,
    gs,
    gk,
    gt,
    sem,
):
    rows = lo_i.shape[1] // BANDS
    pairs = [(gs, gs_h), (gk, gk_h), (gt, gt_h)]
    for p in range(BANDS):
        band = (0, pl.ds(p * rows, rows))
        pairs += [(s.at[band], d.at[band]) for s, d in ((lo_i, lo_h), (gm_i, gm_h), (pc_i, pc_h))]
    copies = [pltpu.make_async_copy(s, d, sem.at[n]) for n, (s, d) in enumerate(pairs)]
    for c in copies[3:]:
        c.start()
    gs[...] = small[:, :W]
    gk[...] = small[:, 2 * W : 5 * W]
    quarter = lax.broadcasted_iota(jnp.int32, (8, 2 * W), 1) // (W // 2)
    for n in range(2):
        gt[n] = jnp.sum(jnp.where(quarter == 2 + n, small[:8, : 2 * W], 0.0))
    for c in copies[:3]:
        c.start()
    for c in copies:
        c.wait()


def per_device(N, ND, node, pool, cot, w, sharp, maps):
    _, pts, width = node.shape
    H = sharp.shape[0]
    QN = H // Q
    W2 = W // 2
    R = W // ND
    any_ = pl.BlockSpec(memory_space=pl.ANY)
    vmem = pl.BlockSpec(memory_space=pltpu.VMEM)
    big = jax.ShapeDtypeStruct((1, pts, width), bf16)
    dma = pltpu.SemaphoreType.DMA
    node, pool, cot, w, sharp, maps = (
        pltpu.with_memory_space_constraint(a, pltpu.HBM) for a in (node, pool, cot, w, sharp, maps)
    )
    lo, gm, pc, small = pl.pallas_call(
        functools.partial(kernel, N, ND, H),
        out_shape=(big, big, big, jax.ShapeDtypeStruct((R, 6 * W), f32)),
        in_specs=[any_] * 6,
        out_specs=[vmem] * 4,
        scratch_shapes=[
            pltpu.VMEM((pts, width), bf16),
            pltpu.VMEM((pts, width), bf16),
            pltpu.VMEM((pts, width), bf16),
            pltpu.VMEM((W, W), bf16),
            pltpu.SMEM((H,), f32),
            pltpu.VMEM((W, 3 * W), f32),
            pltpu.VMEM((width, pts), f32),
            pltpu.VMEM((width, pts), f32),
            pltpu.VMEM((width, pts), bf16),
            pltpu.VMEM((pts, width), bf16),
            pltpu.VMEM((width, pts), bf16),
            pltpu.VMEM((width, pts), f32),
            pltpu.VMEM((QW, QW), bf16),
            pltpu.VMEM((QN, QW, QW), bf16),
            pltpu.VMEM((QN, QW, QW), bf16),
            pltpu.VMEM((2, H, W2 + 8, 2 * W), f32),
            pltpu.VMEM((2, 2, N, W2 + 8, 2 * W), f32),
            pltpu.VMEM((2, 2, N, W2 + 8, 2 * W), f32),
            pltpu.VMEM((2, H, W2 + 8, 2 * W), f32),
            pltpu.VMEM((2, W, 2 * W), f32),
            pltpu.VMEM((H // 2, 8, 2 * W), f32),
            pltpu.VMEM((ND, R, 4 * W), f32),
            pltpu.VMEM((ND, R, 2 * W), f32),
            pltpu.VMEM((3, max(N, ND), R, 4 * W), f32),
            pltpu.VMEM((3, max(N, ND), R, 2 * W), f32),
            dma((3, QN)),
            dma((3,)),
            dma((2,)),
            dma((2, 2)),
            dma((2,)),
            dma((2, 2)),
            dma((2,)),
            dma((2, 2)),
            dma((3,)),
            dma((3,)),
            dma((3,)),
            dma((3,)),
        ],
        compiler_params=pltpu.CompilerParams(
            collective_id=0, has_side_effects=True, vmem_limit_bytes=VMEM_LIMIT
        ),
    )(node, pool, cot, w, sharp, maps)
    each = H // ND
    return pl.pallas_call(
        finish_kernel,
        out_shape=(
            big,
            big,
            big,
            jax.ShapeDtypeStruct((R, W), f32),
            jax.ShapeDtypeStruct((each,), f32),
            jax.ShapeDtypeStruct((R, 3 * W), f32),
        ),
        in_specs=[vmem] * 4,
        out_specs=[any_] * 6,
        scratch_shapes=[
            pltpu.VMEM((R, W), f32),
            pltpu.VMEM((R, 3 * W), f32),
            pltpu.SMEM((each,), f32),
            dma((3 + 3 * BANDS,)),
        ],
        compiler_params=pltpu.CompilerParams(vmem_limit_bytes=VMEM_LIMIT),
    )(lo, gm, pc, small)


def solution(mesh):
    N = int(round(mesh.shape["point"] ** 0.5))
    ND = mesh.shape["dp"]
    big = P("dp", "point", None)
    return jax.shard_map(
        functools.partial(per_device, N, ND),
        mesh=mesh,
        in_specs=(big, big, big, P(), P(), P()),
        out_specs=(big, big, big, P("dp", None), P("dp"), P("dp", None)),
        check_vma=False,
    )
```

```python
import functools

import jax
import jax.numpy as jnp
from jax import lax
from jax.experimental import pallas as pl
from jax.experimental.pallas import tpu as pltpu
from jax.sharding import PartitionSpec as P

epsilon = 1e-05
f32 = jnp.float32
bf16 = jnp.bfloat16
W = 64
Q = 4
QW = Q * W
BANDS = 1
VMEM_LIMIT = 40 * 1024 * 1024
NN = (((1,), (0,)), ((), ()))
NT = (((1,), (1,)), ((), ()))


def bdot(a, b, dims=NN):
    return lax.dot_general(a, b, dims, preferred_element_type=f32)


def hdot(a, b, dims=NN):
    ah, bh = a.astype(bf16), b.astype(bf16)
    al, bl = (a - ah.astype(f32)).astype(bf16), (b - bh.astype(f32)).astype(bf16)
    return bdot(ah, bh, dims) + (bdot(ah, bl, dims) + bdot(al, bh, dims))


def swap_halves(x):
    return pltpu.roll(x, W, 1)


def kernel(
    N,
    ND,
    H,
    node_h,
    pool_h,
    cot_h,
    w_h,
    sharp_h,
    maps_h,
    lo_ref,
    gm_ref,
    pc_ref,
    small_ref,
    node,
    pool,
    cot,
    w_ref,
    sharp_ref,
    maps_ref,
    zed,
    sl,
    slt,
    slb,
    glt,
    gpart,
    bt,
    mbs,
    gbs,
    send1,
    recv1,
    recv2,
    res,
    acc,
    tpart,
    tgrad,
    fin,
    tred,
    fred,
    in_sem,
    par_sem,
    s1,
    r1,
    s2,
    r2,
    s3,
    r3,
    st,
    rt,
    sf,
    rf,
):
    QN = H // Q
    W2 = W // 2
    R = W // ND
    PTS = node.shape[0]
    point = lax.axis_index("point")
    me_d = lax.axis_index("dp")
    me_y = point // N
    me_z = point % N

    def first(f):
        return jnp.where(f == 0, me_y, me_z) if not isinstance(f, int) else (me_y, me_z)[f]

    def second(f):
        return jnp.where(f == 0, me_z, me_y) if not isinstance(f, int) else (me_z, me_y)[f]

    def place(f, i, j):
        if isinstance(f, int):
            return i * N + j if f == 0 else j * N + i
        return jnp.where(f == 0, i * N + j, j * N + i)

    def far_first(n):
        return sorted(range(1, n), key=lambda k: -min(k, n - k))

    def rcopy(src, dst, ssem, rsem, **dev):
        return pltpu.make_async_remote_copy(
            src_ref=src,
            dst_ref=dst,
            send_sem=ssem,
            recv_sem=rsem,
            device_id=dev,
            device_id_type=pl.DeviceIdType.MESH,
        )

    def wait_bytes(like, sem):
        pltpu.make_async_copy(like, like, sem).wait()

    barrier = pltpu.get_barrier_semaphore()

    def greet(**dev):
        pl.semaphore_signal(
            barrier, inc=1, device_id=dev, device_id_type=pl.DeviceIdType.MESH
        )

    for k in far_first(N):
        greet(point=place(0, (me_y + k) % N, me_z))
        greet(point=place(0, me_y, (me_z + k) % N))
    for k in far_first(ND):
        greet(dp=(me_d + k) % ND)

    def order(t):
        return (t % 2) * (QN // 2) + t // 2 if QN > 1 else t

    def fetch(q):
        lanes = pl.ds(pl.multiple_of(q * QW, QW), QW)
        return [
            pltpu.make_async_copy(s.at[0, :, lanes], d.at[:, lanes], in_sem.at[n, q])
            for n, (s, d) in enumerate(((node_h, node), (pool_h, pool), (cot_h, cot)))
        ]

    params = [
        pltpu.make_async_copy(s, d, par_sem.at[n])
        for n, (s, d) in enumerate(((w_h, w_ref), (sharp_h, sharp_ref), (maps_h, maps_ref)))
    ]
    for c in params:
        c.start()
    for t in range(QN):
        for c in fetch(order(t)):
            c.start()

    for c in params:
        c.wait()
    w4 = jnp.concatenate([w_ref[...].astype(f32)] * Q, axis=0)
    w4 = jnp.concatenate([w4] * Q, axis=1)
    row = lax.broadcasted_iota(jnp.int32, (QW, QW), 0)
    col = lax.broadcasted_iota(jnp.int32, (QW, QW), 1)
    w4 = jnp.where(row // W == col // W, w4, 0.0)
    bt[...] = w4.T.astype(bf16)
    low = lax.broadcasted_iota(jnp.int32, (W, 2 * W), 1) < W
    low2 = low[:W2]

    def inv_sharp(h, width):
        return 1.0 / jnp.full((1, width), sharp_ref[h], f32)

    def rows_of(q, i=0, n=QW):
        return pl.ds(pl.multiple_of(q * QW + i * W, W), n)

    def lanes_of(q):
        return pl.ds(pl.multiple_of(q * QW, QW), QW)

    def fold(x, i):
        if i % 2 == 0:
            return jnp.where(low2, x[:W2], swap_halves(x[W2:]))
        return jnp.where(low2, swap_halves(x[:W2]), x[W2:])

    def unfold(x):
        return jnp.concatenate([x[:, :W], swap_halves(x)[:, :W]], axis=0)

    def spread(x, i):
        other = swap_halves(x)
        up, down = (x, other) if i % 2 == 0 else (other, x)
        keep = low2 if i % 2 == 0 else ~low2
        return jnp.concatenate([jnp.where(keep, up, 0.0), jnp.where(keep, down, 0.0)], axis=0)

    def column(row):
        return jnp.broadcast_to(row, (8, 2 * W)).T[:, :1]

    rows_in = (W2 + 1, W2)
    rows_out = (W2, W2 + 1)

    def phase1(s, h, f, i):
        n = pl.ds(0, rows_in[s])
        return rcopy(
            send1.at[s, h, n],
            recv1.at[s, f, first(f), n],
            s1.at[s],
            r1.at[s, f],
            point=place(f, i, second(f)),
        )

    def forward(t):
        q = order(t)
        for c in fetch(q):
            c.wait()
        z = bdot(bt[...], node[:, lanes_of(q)], NT)
        sums = []
        for i in range(Q):
            zh = z[i * W : (i + 1) * W] * inv_sharp(q * Q + i, PTS)
            e = jnp.exp(zh - jnp.max(zh, axis=0, keepdims=True))
            s = e * (1.0 / jnp.sum(e, axis=0, keepdims=True))
            sb = s.astype(bf16)
            zed[rows_of(q, i, W), :] = zh
            sl[rows_of(q, i, W), :] = s
            slt[rows_of(q, i, W), :] = sb
            sums.append(sum(s[:, c : c + 2 * W] for c in range(0, PTS, 2 * W)))
        sq = slt[rows_of(q), :]
        sums = jnp.concatenate(sums, axis=0)
        top = sums.astype(bf16)
        ones = jnp.ones((8, 2 * W), bf16)
        mass = bdot(ones, top, NT) + bdot(ones, (sums - top.astype(f32)).astype(bf16), NT)
        pooled = bdot(sq, pool[:, lanes_of(q)])
        gmixed = bdot(sq, cot[:, lanes_of(q)])
        for i in range(Q):
            r, c = slice(i * W, (i + 1) * W), slice(i // 2 * 2 * W, (i // 2 + 1) * 2 * W)
            m = mass[:, c] if i % 2 == 0 else swap_halves(mass[:, c])
            send1[0, q * Q + i, :W2, :] = fold(pooled[r, c], i)
            send1[0, q * Q + i, W2:, :] = m
            send1[1, q * Q + i, :W2, :] = fold(gmixed[r, c], i)


    for t in range(QN):
        forward(t)

    pl.semaphore_wait(barrier, 2 * (N - 1) + ND - 1)
    for s in range(2):
        for k in far_first(N):
            for f in range(2):
                i = (first(f) + k) % N
                phase1(s, f * N + i, f, i).start()

    def flip(q):
        slb[:, lanes_of(q)] = slt[rows_of(q), :].T

    for q in range(QN):
        flip(q)

    def phase2(s, f, j):
        mine = recv2.at[s, f, second(f), pl.ds(0, rows_in[s])]
        return rcopy(
            mine, mine, s2.at[s], r2.at[s, f], point=place(f, first(f), j)
        )

    def arrived1(s, f):
        h = f * N + first(f)
        own = send1[s, h]
        recv1[s, f, first(f)] = own
        wait_bytes(recv1.at[s, f, pl.ds(0, N - 1), pl.ds(0, rows_in[s])], r1.at[s, f])
        n = rows_in[s]
        part = recv1[s, f, 0, :n, :]
        for i in range(1, N):
            part = part + recv1[s, f, i, :n, :]
        recv2[s, f, second(f), :n, :] = part
        for k in far_first(N):
            phase2(s, f, (second(f) + k) % N).start()

    def arrived2(s, f):
        n = rows_in[s]
        wait_bytes(recv2.at[s, f, pl.ds(0, N - 1), pl.ds(0, n)], r2.at[s, f])
        total = recv2[s, f, 0, :n, :]
        for j in range(1, N):
            total = total + recv2[s, f, j, :n, :]
        return total

    for s in range(2):
        for f in range(2):
            arrived1(s, f)

    for q in range(QN):
        mbs[q] = jnp.zeros((QW, QW), bf16)
        gbs[q] = jnp.zeros((QW, QW), bf16)
    acc[...] = jnp.zeros(acc.shape, f32)

    maps = maps_ref[...]

    def phase3(s, f, i):
        h = f * N + first(f)
        mine = res.at[s, h, pl.ds(0, rows_out[s])]
        return rcopy(
            mine, mine, s3.at[s], r3.at[s, f], point=place(f, i, second(f))
        )

    def send3(s, f):
        for k in far_first(N):
            phase3(s, f, (first(f) + k) % N).start()

    totals = [arrived2(0, f) for f in range(2)]
    mass = jnp.concatenate([total[W2:] for total in totals], axis=0)
    mass = jnp.concatenate([mass, jnp.ones((6, 2 * W), f32)], axis=0).T
    inverse = 1.0 / (jnp.concatenate([mass[:W, :1], mass[:W, 1:2]], axis=0) + epsilon)
    t = jnp.concatenate([unfold(total[:W2]) for total in totals], axis=0) * inverse
    proj = hdot(t, maps)
    query, key, value = proj[:, :W], swap_halves(proj[:, : 2 * W])[:, :W], proj[:, 2 * W :]
    score = hdot(query, key, NT) * W**-0.5
    row = lax.broadcasted_iota(jnp.int32, (2 * W, 2 * W), 0)
    col = lax.broadcasted_iota(jnp.int32, (2 * W, 2 * W), 1)
    score = jnp.where(row // W == col // W, score, -jnp.inf)
    e = jnp.exp(score - jnp.max(score, axis=1, keepdims=True))
    attn = e / jnp.sum(e, axis=1, keepdims=True)
    mixed = hdot(attn, value).astype(bf16).astype(f32)
    for f in range(2):
        res[0, f * N + first(f), :W2, :] = jnp.concatenate(
            [mixed[f * W : f * W + W2], mixed[f * W + W2 : (f + 1) * W]], axis=1
        )
        send3(0, f)

    gmix = jnp.concatenate([unfold(arrived2(1, f)) for f in range(2)], axis=0)
    gattn = hdot(gmix, value, NT)
    gvalue = hdot(attn.T, gmix)
    gscore = attn * (gattn - jnp.sum(attn * gattn, axis=1, keepdims=True)) * W**-0.5
    gquery = hdot(gscore, key)
    gkey = hdot(gscore.T, query)
    gproj = jnp.concatenate([gquery, gkey, gvalue], axis=1)
    gtok = hdot(gproj, maps, NT)
    gpool = (gtok * inverse).astype(bf16).astype(f32)
    gmass = hdot(jnp.ones((8, W), f32), -(gtok * t) * inverse, NT)
    for f in range(2):
        h = f * N + first(f)
        res[1, h, :W2, :] = jnp.concatenate(
            [gpool[f * W : f * W + W2], gpool[f * W + W2 : (f + 1) * W]], axis=1
        )
        here, there = (gmass, swap_halves(gmass)) if f == 0 else (swap_halves(gmass), gmass)
        even = (jnp.zeros((8, 2 * W), jnp.int32) + h) % 2 == 0
        res[1, h, W2:, :] = jnp.where(
            even, jnp.where(low[:8], here, 0.0), jnp.where(low[:8], 0.0, there)
        )
        send3(1, f)

    def all_of(buf, ssem, rsem):
        axes = ((me_d, ND), (me_z, N), (me_y, N))

        def dev(stage, k):
            if stage == 0:
                return {"dp": k}
            return {"point": place(0, me_y, k) if stage == 1 else place(0, k, me_z)}

        def copy(stage, k, src):
            me = axes[stage][0]
            return rcopy(
                src, buf.at[stage, me], ssem.at[stage], rsem.at[stage], **dev(stage, k)
            )

        def send(stage, source):
            me, n = axes[stage]
            for k in far_first(n):
                k = (me + k) % n
                copy(stage, k, source(k)).start()

        def receive(stage):
            me, n = axes[stage]
            wait_bytes(buf.at[stage, pl.ds(0, n - 1)], rsem.at[stage])
            total = buf[stage, 0]
            for k in range(1, n):
                total = total + buf[stage, k]
            return total

        def begin(source):
            buf[0, me_d] = source[me_d]
            send(0, lambda k: source.at[k])

        def onward(stage):
            total = receive(stage - 1)
            me = axes[stage][0]
            buf[stage, me] = total
            send(stage, lambda k: buf.at[stage, me])

        def finish():
            return receive(2)

        def drain():
            for stage in range(3):
                n = axes[stage][1]
                wait_bytes(buf.at[stage, pl.ds(0, n - 1)], ssem.at[stage])

        return begin, onward, finish, drain

    t_begin, t_onward, t_finish, t_drain = all_of(tred, st, rt)
    f_begin, f_onward, f_finish, f_drain = all_of(fred, sf, rf)

    tg = hdot(t.T, gproj) * (1.0 / N)
    tg = jnp.concatenate([tg, jnp.zeros((W, W), f32)], axis=1)
    for d in range(ND):
        tgrad[d] = tg[d * R : (d + 1) * R]
    t_begin(tgrad)

    def halves(s, body):
        for f in range(2):
            wait_bytes(res.at[s, pl.ds(0, N - 1), pl.ds(0, rows_out[s])], r3.at[s, f])
            if QN > 1:
                for q in range(f * (QN // 2), (f + 1) * (QN // 2)):
                    body(q)
        if QN == 1:
            body(0)

    def pair(i):
        return slice(i // 2 * 2 * W, (i // 2 + 1) * 2 * W)

    def with_mixed(q):
        for i in range(Q):
            mbs[q, i * W : (i + 1) * W, pair(i)] = spread(res[0, q * Q + i, :W2, :], i).astype(bf16)
        gpart[rows_of(q), :] = bdot(mbs[q], cot[:, lanes_of(q)], NT)
        lo_ref[0, :, lanes_of(q)] = bdot(slb[:, lanes_of(q)], mbs[q]).astype(bf16)

    halves(0, with_mixed)
    t_onward(1)

    quarter = lax.broadcasted_iota(jnp.int32, (8, 2 * W), 1) // W2

    def backward(q):
        cols = []
        for i in range(Q):
            gbs[q, i * W : (i + 1) * W, pair(i)] = spread(res[1, q * Q + i, :W2, :], i).astype(bf16)
            if i % 2 == 0:
                cols.append(
                    column(
                        res[1, q * Q + i, W2 : W2 + 1, :] + res[1, q * Q + i + 1, W2 : W2 + 1, :]
                    )
                )
        part = None
        gq = gpart[rows_of(q), :] + bdot(gbs[q], pool[:, lanes_of(q)], NT)
        for i in range(Q):
            h = q * Q + i
            s = sl[rows_of(q, i, W), :]
            g = gq[i * W : (i + 1) * W] + cols[i // 2][i % 2 * W : (i % 2 + 1) * W]
            sg = s * g
            gz = sg - s * jnp.sum(sg, axis=0, keepdims=True)
            glt[rows_of(q, i, W), :] = (gz * inv_sharp(h, PTS)).astype(bf16)
            tz = gz * zed[rows_of(q, i, W), :]
            tz = jnp.sum(tz.reshape(W // 8, 8, PTS), axis=0)
            tz = sum(tz[:, c : c + 2 * W] for c in range(0, PTS, 2 * W))
            tz = tz + swap_halves(tz)
            tz = (tz + pltpu.roll(tz, W2, 1)) * inv_sharp(h, 2 * W)
            part = jnp.where(quarter == 2 + i % 2, -tz, part if i % 2 else 0.0)
            if i % 2:
                tpart[h // 2] = part
        gs = bdot(glt[rows_of(q), :], node[:, lanes_of(q)])
        for i in range(Q):
            acc[i % 2] += gs[i * W : (i + 1) * W, pair(i)]

    halves(1, backward)

    gst = jnp.where(low, acc[0] + swap_halves(acc[1]), 0.0)
    gst = jnp.concatenate([gst, jnp.zeros((W, 2 * W), f32)], axis=0).T[:W]
    for d in range(ND):
        fin[d] = gst[d * R : (d + 1) * R]
        fin[d, :8, :] = fin[d, :8, :] + tpart[d]
    f_begin(fin)

    def outputs(q):
        gl = glt[rows_of(q), :].T
        gm_ref[0, :, lanes_of(q)] = bdot(gl, bt[...]).astype(bf16)
        pc_ref[0, :, lanes_of(q)] = bdot(slb[:, lanes_of(q)], gbs[q]).astype(bf16)

    t_onward(2)
    for q in range(QN):
        outputs(q)
    f_onward(1)
    for s in range(2):
        wait_bytes(send1.at[s, pl.ds(0, 2 * N - 2), pl.ds(0, rows_in[s])], s1.at[s])
        wait_bytes(recv2.at[s, :, pl.ds(0, N - 1), pl.ds(0, rows_in[s])], s2.at[s])
        wait_bytes(res.at[s, pl.ds(0, 2 * N - 2), pl.ds(0, rows_out[s])], s3.at[s])
    f_onward(2)
    small_ref[:, 2 * W :] = t_finish()
    t_drain()
    small_ref[:, : 2 * W] = f_finish()
    f_drain()


def finish_kernel(
    lo_i,
    gm_i,
    pc_i,
    small,
    lo_h,
    gm_h,
    pc_h,
    gs_h,
    gt_h,
    gk_h,
    gs,
    gk,
    gt,
    sem,
):
    rows = lo_i.shape[1] // BANDS
    pairs = [(gs, gs_h), (gk, gk_h), (gt, gt_h)]
    for p in range(BANDS):
        band = (0, pl.ds(p * rows, rows))
        pairs += [(s.at[band], d.at[band]) for s, d in ((lo_i, lo_h), (gm_i, gm_h), (pc_i, pc_h))]
    copies = [pltpu.make_async_copy(s, d, sem.at[n]) for n, (s, d) in enumerate(pairs)]
    for c in copies[3:]:
        c.start()
    gs[...] = small[:, :W]
    gk[...] = small[:, 2 * W : 5 * W]
    quarter = lax.broadcasted_iota(jnp.int32, (8, 2 * W), 1) // (W // 2)
    for n in range(2):
        gt[n] = jnp.sum(jnp.where(quarter == 2 + n, small[:8, : 2 * W], 0.0))
    for c in copies[:3]:
        c.start()
    for c in copies:
        c.wait()


def per_device(N, ND, node, pool, cot, w, sharp, maps):
    _, pts, width = node.shape
    H = sharp.shape[0]
    QN = H // Q
    W2 = W // 2
    R = W // ND
    any_ = pl.BlockSpec(memory_space=pl.ANY)
    vmem = pl.BlockSpec(memory_space=pltpu.VMEM)
    big = jax.ShapeDtypeStruct((1, pts, width), bf16)
    dma = pltpu.SemaphoreType.DMA
    node, pool, cot, w, sharp, maps = (
        pltpu.with_memory_space_constraint(a, pltpu.HBM) for a in (node, pool, cot, w, sharp, maps)
    )
    lo, gm, pc, small = pl.pallas_call(
        functools.partial(kernel, N, ND, H),
        out_shape=(big, big, big, jax.ShapeDtypeStruct((R, 6 * W), f32)),
        in_specs=[any_] * 6,
        out_specs=[vmem] * 4,
        scratch_shapes=[
            pltpu.VMEM((pts, width), bf16),
            pltpu.VMEM((pts, width), bf16),
            pltpu.VMEM((pts, width), bf16),
            pltpu.VMEM((W, W), bf16),
            pltpu.SMEM((H,), f32),
            pltpu.VMEM((W, 3 * W), f32),
            pltpu.VMEM((width, pts), f32),
            pltpu.VMEM((width, pts), f32),
            pltpu.VMEM((width, pts), bf16),
            pltpu.VMEM((pts, width), bf16),
            pltpu.VMEM((width, pts), bf16),
            pltpu.VMEM((width, pts), f32),
            pltpu.VMEM((QW, QW), bf16),
            pltpu.VMEM((QN, QW, QW), bf16),
            pltpu.VMEM((QN, QW, QW), bf16),
            pltpu.VMEM((2, H, W2 + 8, 2 * W), f32),
            pltpu.VMEM((2, 2, N, W2 + 8, 2 * W), f32),
            pltpu.VMEM((2, 2, N, W2 + 8, 2 * W), f32),
            pltpu.VMEM((2, H, W2 + 8, 2 * W), f32),
            pltpu.VMEM((2, W, 2 * W), f32),
            pltpu.VMEM((H // 2, 8, 2 * W), f32),
            pltpu.VMEM((ND, R, 4 * W), f32),
            pltpu.VMEM((ND, R, 2 * W), f32),
            pltpu.VMEM((3, max(N, ND), R, 4 * W), f32),
            pltpu.VMEM((3, max(N, ND), R, 2 * W), f32),
            dma((3, QN)),
            dma((3,)),
            dma((2,)),
            dma((2, 2)),
            dma((2,)),
            dma((2, 2)),
            dma((2,)),
            dma((2, 2)),
            dma((3,)),
            dma((3,)),
            dma((3,)),
            dma((3,)),
        ],
        compiler_params=pltpu.CompilerParams(
            collective_id=0, has_side_effects=True, vmem_limit_bytes=VMEM_LIMIT
        ),
    )(node, pool, cot, w, sharp, maps)
    each = H // ND
    return pl.pallas_call(
        finish_kernel,
        out_shape=(
            big,
            big,
            big,
            jax.ShapeDtypeStruct((R, W), f32),
            jax.ShapeDtypeStruct((each,), f32),
            jax.ShapeDtypeStruct((R, 3 * W), f32),
        ),
        in_specs=[vmem] * 4,
        out_specs=[any_] * 6,
        scratch_shapes=[
            pltpu.VMEM((R, W), f32),
            pltpu.VMEM((R, 3 * W), f32),
            pltpu.SMEM((each,), f32),
            dma((3 + 3 * BANDS,)),
        ],
        compiler_params=pltpu.CompilerParams(vmem_limit_bytes=VMEM_LIMIT),
    )(lo, gm, pc, small)


def solution(mesh):
    N = int(round(mesh.shape["point"] ** 0.5))
    ND = mesh.shape["dp"]
    big = P("dp", "point", None)
    return jax.shard_map(
        functools.partial(per_device, N, ND),
        mesh=mesh,
        in_specs=(big, big, big, P(), P(), P()),
        out_specs=(big, big, big, P("dp", None), P("dp"), P("dp", None)),
        check_vma=False,
    )
```

```python
import functools

import jax
import jax.numpy as jnp
from jax import lax
from jax.experimental import pallas as pl
from jax.experimental.pallas import tpu as pltpu
from jax.sharding import PartitionSpec as P

epsilon = 1e-05
f32 = jnp.float32
bf16 = jnp.bfloat16
W = 64
Q = 4
QW = Q * W
BANDS = 1
VMEM_LIMIT = 40 * 1024 * 1024
NN = (((1,), (0,)), ((), ()))
NT = (((1,), (1,)), ((), ()))


def bdot(a, b, dims=NN):
    return lax.dot_general(a, b, dims, preferred_element_type=f32)


def hdot(a, b, dims=NN):
    ah, bh = a.astype(bf16), b.astype(bf16)
    al, bl = (a - ah.astype(f32)).astype(bf16), (b - bh.astype(f32)).astype(bf16)
    return bdot(ah, bh, dims) + (bdot(ah, bl, dims) + bdot(al, bh, dims))


def swap_halves(x):
    return pltpu.roll(x, W, 1)


def kernel(
    N,
    ND,
    H,
    node_h,
    pool_h,
    cot_h,
    w_h,
    sharp_h,
    maps_h,
    lo_ref,
    gm_ref,
    pc_ref,
    small_ref,
    node,
    pool,
    cot,
    w_ref,
    sharp_ref,
    maps_ref,
    zed,
    sl,
    slt,
    slb,
    glt,
    nodet,
    gpart,
    bt,
    mbs,
    gbs,
    send1,
    recv1,
    recv2,
    res,
    tpart,
    tgrad,
    fin,
    tred,
    fred,
    in_sem,
    par_sem,
    s1,
    r1,
    s2,
    r2,
    s3,
    r3,
    st,
    rt,
    sf,
    rf,
):
    QN = H // Q
    W2 = W // 2
    R = W // ND
    PTS = node.shape[0]
    point = lax.axis_index("point")
    me_d = lax.axis_index("dp")
    me_y = point // N
    me_z = point % N

    def first(f):
        return jnp.where(f == 0, me_y, me_z) if not isinstance(f, int) else (me_y, me_z)[f]

    def second(f):
        return jnp.where(f == 0, me_z, me_y) if not isinstance(f, int) else (me_z, me_y)[f]

    def place(f, i, j):
        if isinstance(f, int):
            return i * N + j if f == 0 else j * N + i
        return jnp.where(f == 0, i * N + j, j * N + i)

    def far_first(n):
        return sorted(range(1, n), key=lambda k: -min(k, n - k))

    def rcopy(src, dst, ssem, rsem, **dev):
        return pltpu.make_async_remote_copy(
            src_ref=src,
            dst_ref=dst,
            send_sem=ssem,
            recv_sem=rsem,
            device_id=dev,
            device_id_type=pl.DeviceIdType.MESH,
        )

    def wait_bytes(like, sem):
        pltpu.make_async_copy(like, like, sem).wait()

    barrier = pltpu.get_barrier_semaphore()

    def greet(**dev):
        pl.semaphore_signal(
            barrier, inc=1, device_id=dev, device_id_type=pl.DeviceIdType.MESH
        )

    def greet_ring(steps):
        for k in steps:
            greet(point=place(0, (me_y + k) % N, me_z))
            greet(point=place(0, me_y, (me_z + k) % N))

    greet_ring(far_first(N)[:3])

    inputs = [
        pltpu.make_async_copy(s.at[0], d, in_sem.at[n])
        for n, (s, d) in enumerate(((node_h, node), (pool_h, pool), (cot_h, cot)))
    ]
    params = [
        pltpu.make_async_copy(s, d, par_sem.at[n])
        for n, (s, d) in enumerate(((w_h, w_ref), (sharp_h, sharp_ref), (maps_h, maps_ref)))
    ]
    for c in params[:2] + inputs:
        c.start()
    greet_ring(far_first(N)[3:])
    for k in far_first(ND):
        greet(dp=(me_d + k) % ND)
    params[2].start()
    for c in params[:2]:
        c.wait()
    w4 = jnp.concatenate([w_ref[...].astype(f32)] * Q, axis=0)
    w4 = jnp.concatenate([w4] * Q, axis=1)
    row = lax.broadcasted_iota(jnp.int32, (QW, QW), 0)
    col = lax.broadcasted_iota(jnp.int32, (QW, QW), 1)
    w4 = jnp.where(row // W == col // W, w4, 0.0)
    bt[...] = w4.T.astype(bf16)
    low = lax.broadcasted_iota(jnp.int32, (W, 2 * W), 1) < W
    low2 = low[:W2]

    def inv_sharp(h, width):
        return 1.0 / jnp.full((1, width), sharp_ref[h], f32)

    def rows_of(q, i=0, n=QW):
        return pl.ds(pl.multiple_of(q * QW + i * W, W), n)

    def lanes_of(q):
        return pl.ds(pl.multiple_of(q * QW, QW), QW)

    def fold(x, i):
        if i % 2 == 0:
            return jnp.where(low2, x[:W2], swap_halves(x[W2:]))
        return jnp.where(low2, swap_halves(x[:W2]), x[W2:])

    def unfold(x):
        return jnp.concatenate([x[:, :W], swap_halves(x)[:, :W]], axis=0)

    def spread(x, i):
        other = swap_halves(x)
        up, down = (x, other) if i % 2 == 0 else (other, x)
        keep = low2 if i % 2 == 0 else ~low2
        return jnp.concatenate([jnp.where(keep, up, 0.0), jnp.where(keep, down, 0.0)], axis=0)

    def column(row):
        return jnp.broadcast_to(row, (8, 2 * W)).T[:, :1]

    rows_in = (W2 + 1, W2)
    rows_out = (W2, W2 + 1)

    def phase1(s, h, f, i):
        n = pl.ds(0, rows_in[s])
        return rcopy(
            send1.at[s, h, n],
            recv1.at[s, f, first(f), n],
            s1.at[s],
            r1.at[s, f],
            point=place(f, i, second(f)),
        )

    def soften(q, z):
        sums = []
        for i in range(Q):
            zh = z[i * W : (i + 1) * W] * inv_sharp(q * Q + i, PTS)
            e = jnp.exp(zh - jnp.max(zh, axis=0, keepdims=True))
            s = e * (1.0 / jnp.sum(e, axis=0, keepdims=True))
            sb = s.astype(bf16)
            zed[rows_of(q, i, W), :] = zh
            sl[rows_of(q, i, W), :] = s
            slt[rows_of(q, i, W), :] = sb
            sums.append(sum(s[:, c : c + 2 * W] for c in range(0, PTS, 2 * W)))
        return sums

    def gather(q, sums):
        sq = slt[rows_of(q), :]
        sums = jnp.concatenate(sums, axis=0)
        top = sums.astype(bf16)
        ones = jnp.ones((8, 2 * W), bf16)
        mass = bdot(ones, top, NT) + bdot(ones, (sums - top.astype(f32)).astype(bf16), NT)
        pooled = bdot(sq, pool[:, lanes_of(q)])
        gmixed = bdot(sq, cot[:, lanes_of(q)])
        for i in range(Q):
            r, c = slice(i * W, (i + 1) * W), slice(i // 2 * 2 * W, (i // 2 + 1) * 2 * W)
            m = mass[:, c] if i % 2 == 0 else swap_halves(mass[:, c])
            send1[0, q * Q + i, :W2, :] = fold(pooled[r, c], i)
            send1[0, q * Q + i, W2:, :] = m
            send1[1, q * Q + i, :W2, :] = fold(gmixed[r, c], i)


    inputs[0].wait()
    zs = [bdot(bt[...], node[:, lanes_of(q)], NT) for q in range(QN)]
    sums_of = [soften(q, zs[q]) for q in range(QN)]
    for c in inputs[1:]:
        c.wait()
    for q in range(QN):
        gather(q, sums_of[q])

    pl.semaphore_wait(barrier, 2 * (N - 1) + ND - 1)
    for s in range(2):
        for k in far_first(N):
            for f in range(2):
                i = (first(f) + k) % N
                phase1(s, f * N + i, f, i).start()

    for q in range(QN):
        slb[:, lanes_of(q)] = slt[rows_of(q), :].T
        nodet[rows_of(q), :] = node[:, lanes_of(q)].T
        mbs[q] = jnp.zeros((QW, QW), bf16)
        gbs[q] = jnp.zeros((QW, QW), bf16)

    def phase2(s, f, j):
        mine = recv2.at[s, f, second(f), pl.ds(0, rows_in[s])]
        return rcopy(
            mine, mine, s2.at[s], r2.at[s, f], point=place(f, first(f), j)
        )

    def arrived1(s, f):
        h = f * N + first(f)
        own = send1[s, h]
        recv1[s, f, first(f)] = own
        wait_bytes(recv1.at[s, f, pl.ds(0, N - 1), pl.ds(0, rows_in[s])], r1.at[s, f])
        n = rows_in[s]
        part = recv1[s, f, 0, :n, :]
        for i in range(1, N):
            part = part + recv1[s, f, i, :n, :]
        recv2[s, f, second(f), :n, :] = part
        for k in far_first(N):
            phase2(s, f, (second(f) + k) % N).start()

    def arrived2(s, f):
        n = rows_in[s]
        wait_bytes(recv2.at[s, f, pl.ds(0, N - 1), pl.ds(0, n)], r2.at[s, f])
        total = recv2[s, f, 0, :n, :]
        for j in range(1, N):
            total = total + recv2[s, f, j, :n, :]
        return total

    for s in range(2):
        for f in range(2):
            arrived1(s, f)

    params[2].wait()
    maps = maps_ref[...]

    def phase3(s, f, i):
        h = f * N + first(f)
        mine = res.at[s, h, pl.ds(0, rows_out[s])]
        return rcopy(
            mine, mine, s3.at[s], r3.at[s, f], point=place(f, i, second(f))
        )

    def send3(s, f):
        for k in far_first(N):
            phase3(s, f, (first(f) + k) % N).start()

    totals = [arrived2(0, f) for f in range(2)]
    mass = jnp.concatenate([total[W2:] for total in totals], axis=0)
    mass = jnp.concatenate([mass, jnp.ones((6, 2 * W), f32)], axis=0).T
    inverse = 1.0 / (jnp.concatenate([mass[:W, :1], mass[:W, 1:2]], axis=0) + epsilon)
    t = jnp.concatenate([unfold(total[:W2]) for total in totals], axis=0) * inverse
    proj = hdot(t, maps)
    query, key, value = proj[:, :W], swap_halves(proj[:, : 2 * W])[:, :W], proj[:, 2 * W :]
    score = hdot(query, key, NT) * W**-0.5
    row = lax.broadcasted_iota(jnp.int32, (2 * W, 2 * W), 0)
    col = lax.broadcasted_iota(jnp.int32, (2 * W, 2 * W), 1)
    score = jnp.where(row // W == col // W, score, -jnp.inf)
    e = jnp.exp(score - jnp.max(score, axis=1, keepdims=True))
    attn = e / jnp.sum(e, axis=1, keepdims=True)
    mixed = hdot(attn, value).astype(bf16).astype(f32)
    for f in range(2):
        res[0, f * N + first(f), :W2, :] = jnp.concatenate(
            [mixed[f * W : f * W + W2], mixed[f * W + W2 : (f + 1) * W]], axis=1
        )
        send3(0, f)

    gmix = jnp.concatenate([unfold(arrived2(1, f)) for f in range(2)], axis=0)
    gattn = hdot(gmix, value, NT)
    gvalue = hdot(attn.T, gmix)
    gscore = attn * (gattn - jnp.sum(attn * gattn, axis=1, keepdims=True)) * W**-0.5
    gquery = hdot(gscore, key)
    gkey = hdot(gscore.T, query)
    gproj = jnp.concatenate([gquery, gkey, gvalue], axis=1)
    gtok = hdot(gvalue, maps[:, 2 * W :], NT) + hdot(gproj[:, : 2 * W], maps[:, : 2 * W], NT)
    gpool = (gtok * inverse).astype(bf16).astype(f32)
    gmass = hdot(jnp.ones((8, 3 * W), f32), -(gproj * proj) * inverse, NT)
    for f in range(2):
        h = f * N + first(f)
        res[1, h, :W2, :] = jnp.concatenate(
            [gpool[f * W : f * W + W2], gpool[f * W + W2 : (f + 1) * W]], axis=1
        )
        here, there = (gmass, swap_halves(gmass)) if f == 0 else (swap_halves(gmass), gmass)
        even = (jnp.zeros((8, 2 * W), jnp.int32) + h) % 2 == 0
        res[1, h, W2:, :] = jnp.where(
            even, jnp.where(low[:8], here, 0.0), jnp.where(low[:8], 0.0, there)
        )
        send3(1, f)

    def all_of(buf, ssem, rsem):
        axes = ((me_d, ND), (me_z, N), (me_y, N))

        def dev(stage, k):
            if stage == 0:
                return {"dp": k}
            return {"point": place(0, me_y, k) if stage == 1 else place(0, k, me_z)}

        def copy(stage, k, src):
            me = axes[stage][0]
            return rcopy(
                src, buf.at[stage, me], ssem.at[stage], rsem.at[stage], **dev(stage, k)
            )

        def send(stage, source):
            me, n = axes[stage]
            for k in far_first(n):
                k = (me + k) % n
                copy(stage, k, source(k)).start()

        def receive(stage):
            me, n = axes[stage]
            wait_bytes(buf.at[stage, pl.ds(0, n - 1)], rsem.at[stage])
            total = buf[stage, 0]
            for k in range(1, n):
                total = total + buf[stage, k]
            return total

        def begin(source):
            buf[0, me_d] = source[me_d]
            send(0, lambda k: source.at[k])

        def onward(stage):
            total = receive(stage - 1)
            me = axes[stage][0]
            buf[stage, me] = total
            send(stage, lambda k: buf.at[stage, me])

        def finish():
            return receive(2)

        def drain():
            for stage in range(3):
                n = axes[stage][1]
                wait_bytes(buf.at[stage, pl.ds(0, n - 1)], ssem.at[stage])

        return begin, onward, finish, drain

    t_begin, t_onward, t_finish, t_drain = all_of(tred, st, rt)
    f_begin, f_onward, f_finish, f_drain = all_of(fred, sf, rf)

    tg = hdot(t.T, gproj) * (1.0 / N)
    tg = jnp.concatenate([tg, jnp.zeros((W, W), f32)], axis=1)
    for d in range(ND):
        tgrad[d] = tg[d * R : (d + 1) * R]
    t_begin(tgrad)

    def halves(s, body):
        got = []
        for f in range(2):
            wait_bytes(res.at[s, pl.ds(0, N - 1), pl.ds(0, rows_out[s])], r3.at[s, f])
            if QN > 1:
                got.append(body(range(f * (QN // 2), (f + 1) * (QN // 2))))
        if QN == 1:
            got.append(body(range(1)))
        return got

    def pair(i):
        return slice(i // 2 * 2 * W, (i // 2 + 1) * 2 * W)

    def with_mixed(groups):
        for q in groups:
            for i in range(Q):
                block = spread(res[0, q * Q + i, :W2, :], i)
                mbs[q, i * W : (i + 1) * W, pair(i)] = block.astype(bf16)
        for q in groups:
            gpart[rows_of(q), :] = bdot(mbs[q], cot[:, lanes_of(q)], NT)
        for q in groups:
            lo_ref[0, :, lanes_of(q)] = bdot(slb[:, lanes_of(q)], mbs[q]).astype(bf16)

    halves(0, with_mixed)

    quarter = lax.broadcasted_iota(jnp.int32, (8, 2 * W), 1) // W2

    def backward(groups):
        gqs, cols = {}, {}
        for q in groups:
            cols[q] = []
            for i in range(Q):
                block = spread(res[1, q * Q + i, :W2, :], i)
                gbs[q, i * W : (i + 1) * W, pair(i)] = block.astype(bf16)
                if i % 2 == 0:
                    row = (
                        res[1, q * Q + i, W2 : W2 + 1, :] + res[1, q * Q + i + 1, W2 : W2 + 1, :]
                    )
                    cols[q].append(column(row))
        for q in groups:
            gqs[q] = gpart[rows_of(q), :] + bdot(gbs[q], pool[:, lanes_of(q)], NT)
        for q in groups:
            for i in range(Q):
                h = q * Q + i
                s = sl[rows_of(q, i, W), :]
                g = gqs[q][i * W : (i + 1) * W] + cols[q][i // 2][i % 2 * W : (i % 2 + 1) * W]
                sg = s * g
                gz = sg - s * jnp.sum(sg, axis=0, keepdims=True)
                glt[rows_of(q, i, W), :] = (gz * inv_sharp(h, PTS)).astype(bf16)
                tz = gz * zed[rows_of(q, i, W), :]
                tz = jnp.sum(tz.reshape(W // 8, 8, PTS), axis=0)
                tz = sum(tz[:, c : c + 2 * W] for c in range(0, PTS, 2 * W))
                tz = tz + swap_halves(tz)
                tz = (tz + pltpu.roll(tz, W2, 1)) * inv_sharp(h, 2 * W)
                part = jnp.where(quarter == 2 + i % 2, -tz, part if i % 2 else 0.0)
                if i % 2:
                    tpart[h // 2] = part
        sides = [0.0, 0.0]
        for q in groups:
            gs = bdot(nodet[rows_of(q), :], glt[rows_of(q), :], NT)
            for i in range(Q):
                sides[i % 2] = sides[i % 2] + gs[i * W : (i + 1) * W, pair(i)]
        return sides

    left, right = (sum(x) for x in zip(*halves(1, backward)))

    gst = jnp.where(low, left + swap_halves(right), 0.0)
    for d in range(ND):
        fin[d] = gst[d * R : (d + 1) * R]
        fin[d, :8, :] = fin[d, :8, :] + tpart[d]
    f_begin(fin)

    def outputs(q):
        gl = glt[rows_of(q), :].T
        gm_ref[0, :, lanes_of(q)] = bdot(gl, bt[...]).astype(bf16)
        pc_ref[0, :, lanes_of(q)] = bdot(slb[:, lanes_of(q)], gbs[q]).astype(bf16)

    t_onward(1)
    for q in range(QN):
        outputs(q)
    f_onward(1)
    t_onward(2)
    for s in range(2):
        wait_bytes(send1.at[s, pl.ds(0, 2 * N - 2), pl.ds(0, rows_in[s])], s1.at[s])
        wait_bytes(recv2.at[s, :, pl.ds(0, N - 1), pl.ds(0, rows_in[s])], s2.at[s])
        wait_bytes(res.at[s, pl.ds(0, 2 * N - 2), pl.ds(0, rows_out[s])], s3.at[s])
    f_onward(2)
    small_ref[:, 2 * W :] = t_finish()
    t_drain()
    small_ref[:, : 2 * W] = f_finish()
    f_drain()


def finish_kernel(
    lo_i,
    gm_i,
    pc_i,
    small,
    lo_h,
    gm_h,
    pc_h,
    gs_h,
    gt_h,
    gk_h,
    gs,
    gk,
    gt,
    sem,
):
    rows = lo_i.shape[1] // BANDS
    pairs = [(gs, gs_h), (gk, gk_h), (gt, gt_h)]
    for p in range(BANDS):
        band = (0, pl.ds(p * rows, rows))
        pairs += [(s.at[band], d.at[band]) for s, d in ((lo_i, lo_h), (gm_i, gm_h), (pc_i, pc_h))]
    copies = [pltpu.make_async_copy(s, d, sem.at[n]) for n, (s, d) in enumerate(pairs)]
    for c in copies[3:]:
        c.start()
    gs[...] = small[:, :W]
    gk[...] = small[:, 2 * W : 5 * W]
    quarter = lax.broadcasted_iota(jnp.int32, (8, 2 * W), 1) // (W // 2)
    for n in range(2):
        gt[n] = jnp.sum(jnp.where(quarter == 2 + n, small[:8, : 2 * W], 0.0))
    for c in copies[:3]:
        c.start()
    for c in copies:
        c.wait()


def per_device(N, ND, node, pool, cot, w, sharp, maps):
    _, pts, width = node.shape
    H = sharp.shape[0]
    QN = H // Q
    W2 = W // 2
    R = W // ND
    any_ = pl.BlockSpec(memory_space=pl.ANY)
    vmem = pl.BlockSpec(memory_space=pltpu.VMEM)
    big = jax.ShapeDtypeStruct((1, pts, width), bf16)
    dma = pltpu.SemaphoreType.DMA
    node, pool, cot, w, sharp, maps = (
        pltpu.with_memory_space_constraint(a, pltpu.HBM) for a in (node, pool, cot, w, sharp, maps)
    )
    lo, gm, pc, small = pl.pallas_call(
        functools.partial(kernel, N, ND, H),
        out_shape=(big, big, big, jax.ShapeDtypeStruct((R, 6 * W), f32)),
        in_specs=[any_] * 6,
        out_specs=[vmem] * 4,
        scratch_shapes=[
            pltpu.VMEM((pts, width), bf16),
            pltpu.VMEM((pts, width), bf16),
            pltpu.VMEM((pts, width), bf16),
            pltpu.VMEM((W, W), bf16),
            pltpu.SMEM((H,), f32),
            pltpu.VMEM((W, 3 * W), f32),
            pltpu.VMEM((width, pts), f32),
            pltpu.VMEM((width, pts), f32),
            pltpu.VMEM((width, pts), bf16),
            pltpu.VMEM((pts, width), bf16),
            pltpu.VMEM((width, pts), bf16),
            pltpu.VMEM((width, pts), bf16),
            pltpu.VMEM((width, pts), f32),
            pltpu.VMEM((QW, QW), bf16),
            pltpu.VMEM((QN, QW, QW), bf16),
            pltpu.VMEM((QN, QW, QW), bf16),
            pltpu.VMEM((2, H, W2 + 8, 2 * W), f32),
            pltpu.VMEM((2, 2, N, W2 + 8, 2 * W), f32),
            pltpu.VMEM((2, 2, N, W2 + 8, 2 * W), f32),
            pltpu.VMEM((2, H, W2 + 8, 2 * W), f32),
            pltpu.VMEM((H // 2, 8, 2 * W), f32),
            pltpu.VMEM((ND, R, 4 * W), f32),
            pltpu.VMEM((ND, R, 2 * W), f32),
            pltpu.VMEM((3, max(N, ND), R, 4 * W), f32),
            pltpu.VMEM((3, max(N, ND), R, 2 * W), f32),
            dma((3,)),
            dma((3,)),
            dma((2,)),
            dma((2, 2)),
            dma((2,)),
            dma((2, 2)),
            dma((2,)),
            dma((2, 2)),
            dma((3,)),
            dma((3,)),
            dma((3,)),
            dma((3,)),
        ],
        compiler_params=pltpu.CompilerParams(
            collective_id=0, has_side_effects=True, vmem_limit_bytes=VMEM_LIMIT
        ),
    )(node, pool, cot, w, sharp, maps)
    each = H // ND
    return pl.pallas_call(
        finish_kernel,
        out_shape=(
            big,
            big,
            big,
            jax.ShapeDtypeStruct((R, W), f32),
            jax.ShapeDtypeStruct((each,), f32),
            jax.ShapeDtypeStruct((R, 3 * W), f32),
        ),
        in_specs=[vmem] * 4,
        out_specs=[any_] * 6,
        scratch_shapes=[
            pltpu.VMEM((R, W), f32),
            pltpu.VMEM((R, 3 * W), f32),
            pltpu.SMEM((each,), f32),
            dma((3 + 3 * BANDS,)),
        ],
        compiler_params=pltpu.CompilerParams(vmem_limit_bytes=VMEM_LIMIT),
    )(lo, gm, pc, small)


def solution(mesh):
    N = int(round(mesh.shape["point"] ** 0.5))
    ND = mesh.shape["dp"]
    big = P("dp", "point", None)
    return jax.shard_map(
        functools.partial(per_device, N, ND),
        mesh=mesh,
        in_specs=(big, big, big, P(), P(), P()),
        out_specs=(big, big, big, P("dp", None), P("dp"), P("dp", None)),
        check_vma=False,
    )
```

```python
import functools

import jax
import jax.numpy as jnp
from jax import lax
from jax.experimental import pallas as pl
from jax.experimental.pallas import tpu as pltpu
from jax.sharding import PartitionSpec as P

epsilon = 1e-05
f32 = jnp.float32
bf16 = jnp.bfloat16
W = 64
Q = 4
QW = Q * W
BANDS = 1
VMEM_LIMIT = 40 * 1024 * 1024
NN = (((1,), (0,)), ((), ()))
NT = (((1,), (1,)), ((), ()))


def bdot(a, b, dims=NN):
    return lax.dot_general(a, b, dims, preferred_element_type=f32)


def hdot(a, b, dims=NN):
    ah, bh = a.astype(bf16), b.astype(bf16)
    al, bl = (a - ah.astype(f32)).astype(bf16), (b - bh.astype(f32)).astype(bf16)
    return bdot(ah, bh, dims) + (bdot(ah, bl, dims) + bdot(al, bh, dims))


def swap_halves(x):
    return pltpu.roll(x, W, 1)


def kernel(
    N,
    ND,
    H,
    node_h,
    pool_h,
    cot_h,
    w_h,
    sharp_h,
    maps_h,
    lo_ref,
    gm_ref,
    pc_ref,
    small_ref,
    node,
    pool,
    cot,
    w_ref,
    sharp_ref,
    maps_ref,
    zed,
    sl,
    slt,
    slb,
    glt,
    nodet,
    gpart,
    bt,
    mbs,
    gbs,
    send1,
    recv1,
    recv2,
    res,
    tpart,
    tgrad,
    fin,
    tred,
    fred,
    in_sem,
    par_sem,
    s1,
    r1,
    s2,
    r2,
    s3,
    r3,
    st,
    rt,
    sf,
    rf,
):
    QN = H // Q
    W2 = W // 2
    R = W // ND
    PTS = node.shape[0]
    point = lax.axis_index("point")
    me_d = lax.axis_index("dp")
    me_y = point // N
    me_z = point % N

    def first(f):
        return jnp.where(f == 0, me_y, me_z) if not isinstance(f, int) else (me_y, me_z)[f]

    def second(f):
        return jnp.where(f == 0, me_z, me_y) if not isinstance(f, int) else (me_z, me_y)[f]

    def place(f, i, j):
        if isinstance(f, int):
            return i * N + j if f == 0 else j * N + i
        return jnp.where(f == 0, i * N + j, j * N + i)

    def far_first(n):
        return sorted(range(1, n), key=lambda k: -min(k, n - k))

    def rcopy(src, dst, ssem, rsem, **dev):
        return pltpu.make_async_remote_copy(
            src_ref=src,
            dst_ref=dst,
            send_sem=ssem,
            recv_sem=rsem,
            device_id=dev,
            device_id_type=pl.DeviceIdType.MESH,
        )

    def wait_bytes(like, sem):
        pltpu.make_async_copy(like, like, sem).wait()

    barrier = pltpu.get_barrier_semaphore()

    def greet(**dev):
        pl.semaphore_signal(
            barrier, inc=1, device_id=dev, device_id_type=pl.DeviceIdType.MESH
        )

    def greet_ring(steps):
        for k in steps:
            greet(point=place(0, (me_y + k) % N, me_z))
            greet(point=place(0, me_y, (me_z + k) % N))

    greet_ring(far_first(N)[:3])

    inputs = [
        pltpu.make_async_copy(s.at[0], d, in_sem.at[n])
        for n, (s, d) in enumerate(((node_h, node), (pool_h, pool), (cot_h, cot)))
    ]
    params = [
        pltpu.make_async_copy(s, d, par_sem.at[n])
        for n, (s, d) in enumerate(((w_h, w_ref), (sharp_h, sharp_ref), (maps_h, maps_ref)))
    ]
    for c in params[:2] + inputs:
        c.start()
    greet_ring(far_first(N)[3:])
    for k in far_first(ND):
        greet(dp=(me_d + k) % ND)
    params[2].start()
    for c in params[:2]:
        c.wait()
    w4 = jnp.concatenate([w_ref[...].astype(f32)] * Q, axis=0)
    w4 = jnp.concatenate([w4] * Q, axis=1)
    row = lax.broadcasted_iota(jnp.int32, (QW, QW), 0)
    col = lax.broadcasted_iota(jnp.int32, (QW, QW), 1)
    w4 = jnp.where(row // W == col // W, w4, 0.0)
    bt[...] = w4.T.astype(bf16)
    low = lax.broadcasted_iota(jnp.int32, (W, 2 * W), 1) < W
    low2 = low[:W2]

    def inv_sharp(h, width):
        return 1.0 / jnp.full((1, width), sharp_ref[h], f32)

    def rows_of(q, i=0, n=QW):
        return pl.ds(pl.multiple_of(q * QW + i * W, W), n)

    def lanes_of(q):
        return pl.ds(pl.multiple_of(q * QW, QW), QW)

    def fold(x, i):
        if i % 2 == 0:
            return jnp.where(low2, x[:W2], swap_halves(x[W2:]))
        return jnp.where(low2, swap_halves(x[:W2]), x[W2:])

    def unfold(x):
        return jnp.concatenate([x[:, :W], swap_halves(x)[:, :W]], axis=0)

    def spread(x, i):
        other = swap_halves(x)
        up, down = (x, other) if i % 2 == 0 else (other, x)
        keep = low2 if i % 2 == 0 else ~low2
        return jnp.concatenate([jnp.where(keep, up, 0.0), jnp.where(keep, down, 0.0)], axis=0)

    def column(row):
        return jnp.broadcast_to(row, (8, 2 * W)).T[:, :1]

    rows_in = (W2 + 1, W2)
    rows_out = (W2, W2 + 1)

    def phase1(s, h, f, i):
        n = pl.ds(0, rows_in[s])
        return rcopy(
            send1.at[s, h, n],
            recv1.at[s, f, first(f), n],
            s1.at[s],
            r1.at[s],
            point=place(f, i, second(f)),
        )

    def soften(q, z):
        sums = []
        for i in range(Q):
            zh = z[i * W : (i + 1) * W] * inv_sharp(q * Q + i, PTS)
            e = jnp.exp(zh - jnp.max(zh, axis=0, keepdims=True))
            s = e * (1.0 / jnp.sum(e, axis=0, keepdims=True))
            sb = s.astype(bf16)
            zed[rows_of(q, i, W), :] = zh
            sl[rows_of(q, i, W), :] = s
            slt[rows_of(q, i, W), :] = sb
            sums.append(sum(s[:, c : c + 2 * W] for c in range(0, PTS, 2 * W)))
        return sums

    def gather(q, sums):
        sq = slt[rows_of(q), :]
        sums = jnp.concatenate(sums, axis=0)
        top = sums.astype(bf16)
        ones = jnp.ones((8, 2 * W), bf16)
        mass = bdot(ones, top, NT) + bdot(ones, (sums - top.astype(f32)).astype(bf16), NT)
        pooled = bdot(sq, pool[:, lanes_of(q)])
        gmixed = bdot(sq, cot[:, lanes_of(q)])
        for i in range(Q):
            r, c = slice(i * W, (i + 1) * W), slice(i // 2 * 2 * W, (i // 2 + 1) * 2 * W)
            m = mass[:, c] if i % 2 == 0 else swap_halves(mass[:, c])
            send1[0, q * Q + i, :W2, :] = fold(pooled[r, c], i)
            send1[0, q * Q + i, W2:, :] = m
            send1[1, q * Q + i, :W2, :] = fold(gmixed[r, c], i)


    inputs[0].wait()
    zs = [bdot(bt[...], node[:, lanes_of(q)], NT) for q in range(QN)]
    sums_of = [soften(q, zs[q]) for q in range(QN)]
    for c in inputs[1:]:
        c.wait()
    for q in range(QN):
        gather(q, sums_of[q])

    pl.semaphore_wait(barrier, 2 * (N - 1) + ND - 1)
    for s in range(2):
        for k in far_first(N):
            for f in range(2):
                i = (first(f) + k) % N
                phase1(s, f * N + i, f, i).start()

    for q in range(QN):
        slb[:, lanes_of(q)] = slt[rows_of(q), :].T
        nodet[rows_of(q), :] = node[:, lanes_of(q)].T
        mbs[q] = jnp.zeros((QW, QW), bf16)
        gbs[q] = jnp.zeros((QW, QW), bf16)

    def phase2(s, f, j):
        mine = recv2.at[s, f, second(f), pl.ds(0, rows_in[s])]
        return rcopy(
            mine, mine, s2.at[s], r2.at[s], point=place(f, first(f), j)
        )

    def arrived1(s):
        n = rows_in[s]
        for f in range(2):
            recv1[s, f, first(f)] = send1[s, f * N + first(f)]
        wait_bytes(recv1.at[s, :, pl.ds(0, N - 1), pl.ds(0, n)], r1.at[s])
        for f in range(2):
            part = recv1[s, f, 0, :n, :]
            for i in range(1, N):
                part = part + recv1[s, f, i, :n, :]
            recv2[s, f, second(f), :n, :] = part
        for k in far_first(N):
            for f in range(2):
                phase2(s, f, (second(f) + k) % N).start()

    def arrived2(s):
        n = rows_in[s]
        wait_bytes(recv2.at[s, :, pl.ds(0, N - 1), pl.ds(0, n)], r2.at[s])
        totals = []
        for f in range(2):
            total = recv2[s, f, 0, :n, :]
            for j in range(1, N):
                total = total + recv2[s, f, j, :n, :]
            totals.append(total)
        return totals

    for s in range(2):
        arrived1(s)

    params[2].wait()
    maps = maps_ref[...]

    def phase3(s, f, i):
        h = f * N + first(f)
        mine = res.at[s, h, pl.ds(0, rows_out[s])]
        return rcopy(
            mine, mine, s3.at[s], r3.at[s], point=place(f, i, second(f))
        )

    def send3(s):
        for k in far_first(N):
            for f in range(2):
                phase3(s, f, (first(f) + k) % N).start()

    totals = arrived2(0)
    mass = jnp.concatenate([total[W2:] for total in totals], axis=0)
    mass = jnp.concatenate([mass, jnp.ones((6, 2 * W), f32)], axis=0).T
    inverse = 1.0 / (jnp.concatenate([mass[:W, :1], mass[:W, 1:2]], axis=0) + epsilon)
    t = jnp.concatenate([unfold(total[:W2]) for total in totals], axis=0) * inverse
    proj = hdot(t, maps)
    query, key, value = proj[:, :W], swap_halves(proj[:, : 2 * W])[:, :W], proj[:, 2 * W :]
    score = hdot(query, key, NT) * W**-0.5
    row = lax.broadcasted_iota(jnp.int32, (2 * W, 2 * W), 0)
    col = lax.broadcasted_iota(jnp.int32, (2 * W, 2 * W), 1)
    score = jnp.where(row // W == col // W, score, -jnp.inf)
    e = jnp.exp(score - jnp.max(score, axis=1, keepdims=True))
    attn = e / jnp.sum(e, axis=1, keepdims=True)
    mixed = hdot(attn, value).astype(bf16).astype(f32)
    for f in range(2):
        res[0, f * N + first(f), :W2, :] = jnp.concatenate(
            [mixed[f * W : f * W + W2], mixed[f * W + W2 : (f + 1) * W]], axis=1
        )
    send3(0)

    gmix = jnp.concatenate([unfold(total) for total in arrived2(1)], axis=0)
    gattn = hdot(gmix, value, NT)
    gvalue = hdot(attn.T, gmix)
    gscore = attn * (gattn - jnp.sum(attn * gattn, axis=1, keepdims=True)) * W**-0.5
    gquery = hdot(gscore, key)
    gkey = hdot(gscore.T, query)
    gproj = jnp.concatenate([gquery, gkey, gvalue], axis=1)
    gtok = hdot(gvalue, maps[:, 2 * W :], NT) + hdot(gproj[:, : 2 * W], maps[:, : 2 * W], NT)
    gpool = (gtok * inverse).astype(bf16).astype(f32)
    gmass = hdot(jnp.ones((8, 3 * W), f32), -(gproj * proj) * inverse, NT)
    for f in range(2):
        h = f * N + first(f)
        res[1, h, :W2, :] = jnp.concatenate(
            [gpool[f * W : f * W + W2], gpool[f * W + W2 : (f + 1) * W]], axis=1
        )
        here, there = (gmass, swap_halves(gmass)) if f == 0 else (swap_halves(gmass), gmass)
        even = (jnp.zeros((8, 2 * W), jnp.int32) + h) % 2 == 0
        res[1, h, W2:, :] = jnp.where(
            even, jnp.where(low[:8], here, 0.0), jnp.where(low[:8], 0.0, there)
        )
    send3(1)

    def all_of(buf, ssem, rsem):
        axes = ((me_d, ND), (me_z, N), (me_y, N))

        def dev(stage, k):
            if stage == 0:
                return {"dp": k}
            return {"point": place(0, me_y, k) if stage == 1 else place(0, k, me_z)}

        def copy(stage, k, src):
            me = axes[stage][0]
            return rcopy(
                src, buf.at[stage, me], ssem.at[0], rsem.at[stage], **dev(stage, k)
            )

        def send(stage, source):
            me, n = axes[stage]
            for k in far_first(n):
                k = (me + k) % n
                copy(stage, k, source(k)).start()

        def receive(stage):
            me, n = axes[stage]
            wait_bytes(buf.at[stage, pl.ds(0, n - 1)], rsem.at[stage])
            total = buf[stage, 0]
            for k in range(1, n):
                total = total + buf[stage, k]
            return total

        def begin(source):
            buf[0, me_d] = source[me_d]
            send(0, lambda k: source.at[k])

        def onward(stage):
            total = receive(stage - 1)
            me = axes[stage][0]
            buf[stage, me] = total
            send(stage, lambda k: buf.at[stage, me])

        def finish():
            return receive(2)

        def drain():
            if N == ND:
                wait_bytes(buf.at[:, pl.ds(0, N - 1)], ssem.at[0])
            else:
                raise NotImplementedError

        return begin, onward, finish, drain

    t_begin, t_onward, t_finish, t_drain = all_of(tred, st, rt)
    f_begin, f_onward, f_finish, f_drain = all_of(fred, sf, rf)

    tg = hdot(t.T, gproj) * (1.0 / N)
    tg = jnp.concatenate([tg, jnp.zeros((W, W), f32)], axis=1)
    for d in range(ND):
        tgrad[d] = tg[d * R : (d + 1) * R]
    t_begin(tgrad)

    def await3(s):
        wait_bytes(res.at[s, pl.ds(0, 2 * N - 2), pl.ds(0, rows_out[s])], r3.at[s])

    def pair(i):
        return slice(i // 2 * 2 * W, (i // 2 + 1) * 2 * W)

    def with_mixed(groups):
        for q in groups:
            for i in range(Q):
                block = spread(res[0, q * Q + i, :W2, :], i)
                mbs[q, i * W : (i + 1) * W, pair(i)] = block.astype(bf16)
        for q in groups:
            gpart[rows_of(q), :] = bdot(mbs[q], cot[:, lanes_of(q)], NT)
        for q in groups:
            lo_ref[0, :, lanes_of(q)] = bdot(slb[:, lanes_of(q)], mbs[q]).astype(bf16)

    await3(0)
    with_mixed(range(QN))

    quarter = lax.broadcasted_iota(jnp.int32, (8, 2 * W), 1) // W2

    def backward(groups):
        gqs, cols = {}, {}
        for q in groups:
            cols[q] = []
            for i in range(Q):
                block = spread(res[1, q * Q + i, :W2, :], i)
                gbs[q, i * W : (i + 1) * W, pair(i)] = block.astype(bf16)
                if i % 2 == 0:
                    row = (
                        res[1, q * Q + i, W2 : W2 + 1, :] + res[1, q * Q + i + 1, W2 : W2 + 1, :]
                    )
                    cols[q].append(column(row))
        for q in groups:
            gqs[q] = gpart[rows_of(q), :] + bdot(gbs[q], pool[:, lanes_of(q)], NT)
        for q in groups:
            for i in range(Q):
                h = q * Q + i
                s = sl[rows_of(q, i, W), :]
                g = gqs[q][i * W : (i + 1) * W] + cols[q][i // 2][i % 2 * W : (i % 2 + 1) * W]
                sg = s * g
                gz = sg - s * jnp.sum(sg, axis=0, keepdims=True)
                glt[rows_of(q, i, W), :] = (gz * inv_sharp(h, PTS)).astype(bf16)
                tz = gz * zed[rows_of(q, i, W), :]
                tz = jnp.sum(tz.reshape(W // 8, 8, PTS), axis=0)
                tz = sum(tz[:, c : c + 2 * W] for c in range(0, PTS, 2 * W))
                tz = tz + swap_halves(tz)
                tz = (tz + pltpu.roll(tz, W2, 1)) * inv_sharp(h, 2 * W)
                part = jnp.where(quarter == 2 + i % 2, -tz, part if i % 2 else 0.0)
                if i % 2:
                    tpart[h // 2] = part
        sides = [0.0, 0.0]
        for q in groups:
            gs = bdot(nodet[rows_of(q), :], glt[rows_of(q), :], NT)
            for i in range(Q):
                sides[i % 2] = sides[i % 2] + gs[i * W : (i + 1) * W, pair(i)]
        return sides

    await3(1)
    left, right = backward(range(QN))

    gst = jnp.where(low, left + swap_halves(right), 0.0)
    for d in range(ND):
        fin[d] = gst[d * R : (d + 1) * R]
        fin[d, :8, :] = fin[d, :8, :] + tpart[d]
    f_begin(fin)

    def outputs(q):
        gl = glt[rows_of(q), :].T
        gm_ref[0, :, lanes_of(q)] = bdot(gl, bt[...]).astype(bf16)
        pc_ref[0, :, lanes_of(q)] = bdot(slb[:, lanes_of(q)], gbs[q]).astype(bf16)

    t_onward(1)
    for q in range(QN):
        outputs(q)
    f_onward(1)
    t_onward(2)
    for s in range(2):
        wait_bytes(send1.at[s, pl.ds(0, 2 * N - 2), pl.ds(0, rows_in[s])], s1.at[s])
        wait_bytes(recv2.at[s, :, pl.ds(0, N - 1), pl.ds(0, rows_in[s])], s2.at[s])
        wait_bytes(res.at[s, pl.ds(0, 2 * N - 2), pl.ds(0, rows_out[s])], s3.at[s])
    f_onward(2)
    small_ref[:, 2 * W :] = t_finish()
    t_drain()
    small_ref[:, : 2 * W] = f_finish()
    f_drain()


def finish_kernel(
    lo_i,
    gm_i,
    pc_i,
    small,
    lo_h,
    gm_h,
    pc_h,
    gs_h,
    gt_h,
    gk_h,
    gs,
    gk,
    gt,
    sem,
):
    rows = lo_i.shape[1] // BANDS
    pairs = [(gs, gs_h), (gk, gk_h), (gt, gt_h)]
    for p in range(BANDS):
        band = (0, pl.ds(p * rows, rows))
        pairs += [(s.at[band], d.at[band]) for s, d in ((lo_i, lo_h), (gm_i, gm_h), (pc_i, pc_h))]
    copies = [pltpu.make_async_copy(s, d, sem.at[n]) for n, (s, d) in enumerate(pairs)]
    for c in copies[3:]:
        c.start()
    gs[...] = small[:, :W]
    gk[...] = small[:, 2 * W : 5 * W]
    quarter = lax.broadcasted_iota(jnp.int32, (8, 2 * W), 1) // (W // 2)
    for n in range(2):
        gt[n] = jnp.sum(jnp.where(quarter == 2 + n, small[:8, : 2 * W], 0.0))
    for c in copies[:3]:
        c.start()
    for c in copies:
        c.wait()


def per_device(N, ND, node, pool, cot, w, sharp, maps):
    _, pts, width = node.shape
    H = sharp.shape[0]
    QN = H // Q
    W2 = W // 2
    R = W // ND
    any_ = pl.BlockSpec(memory_space=pl.ANY)
    vmem = pl.BlockSpec(memory_space=pltpu.VMEM)
    big = jax.ShapeDtypeStruct((1, pts, width), bf16)
    dma = pltpu.SemaphoreType.DMA
    node, pool, cot, w, sharp, maps = (
        pltpu.with_memory_space_constraint(a, pltpu.HBM) for a in (node, pool, cot, w, sharp, maps)
    )
    lo, gm, pc, small = pl.pallas_call(
        functools.partial(kernel, N, ND, H),
        out_shape=(big, big, big, jax.ShapeDtypeStruct((R, 6 * W), f32)),
        in_specs=[any_] * 6,
        out_specs=[vmem] * 4,
        scratch_shapes=[
            pltpu.VMEM((pts, width), bf16),
            pltpu.VMEM((pts, width), bf16),
            pltpu.VMEM((pts, width), bf16),
            pltpu.VMEM((W, W), bf16),
            pltpu.SMEM((H,), f32),
            pltpu.VMEM((W, 3 * W), f32),
            pltpu.VMEM((width, pts), f32),
            pltpu.VMEM((width, pts), f32),
            pltpu.VMEM((width, pts), bf16),
            pltpu.VMEM((pts, width), bf16),
            pltpu.VMEM((width, pts), bf16),
            pltpu.VMEM((width, pts), bf16),
            pltpu.VMEM((width, pts), f32),
            pltpu.VMEM((QW, QW), bf16),
            pltpu.VMEM((QN, QW, QW), bf16),
            pltpu.VMEM((QN, QW, QW), bf16),
            pltpu.VMEM((2, H, W2 + 8, 2 * W), f32),
            pltpu.VMEM((2, 2, N, W2 + 8, 2 * W), f32),
            pltpu.VMEM((2, 2, N, W2 + 8, 2 * W), f32),
            pltpu.VMEM((2, H, W2 + 8, 2 * W), f32),
            pltpu.VMEM((H // 2, 8, 2 * W), f32),
            pltpu.VMEM((ND, R, 4 * W), f32),
            pltpu.VMEM((ND, R, 2 * W), f32),
            pltpu.VMEM((3, max(N, ND), R, 4 * W), f32),
            pltpu.VMEM((3, max(N, ND), R, 2 * W), f32),
            dma((3,)),
            dma((3,)),
            dma((2,)),
            dma((2,)),
            dma((2,)),
            dma((2,)),
            dma((2,)),
            dma((2,)),
            dma((1,)),
            dma((3,)),
            dma((1,)),
            dma((3,)),
        ],
        compiler_params=pltpu.CompilerParams(
            collective_id=0, has_side_effects=True, vmem_limit_bytes=VMEM_LIMIT
        ),
    )(node, pool, cot, w, sharp, maps)
    each = H // ND
    return pl.pallas_call(
        finish_kernel,
        out_shape=(
            big,
            big,
            big,
            jax.ShapeDtypeStruct((R, W), f32),
            jax.ShapeDtypeStruct((each,), f32),
            jax.ShapeDtypeStruct((R, 3 * W), f32),
        ),
        in_specs=[vmem] * 4,
        out_specs=[any_] * 6,
        scratch_shapes=[
            pltpu.VMEM((R, W), f32),
            pltpu.VMEM((R, 3 * W), f32),
            pltpu.SMEM((each,), f32),
            dma((3 + 3 * BANDS,)),
        ],
        compiler_params=pltpu.CompilerParams(vmem_limit_bytes=VMEM_LIMIT),
    )(lo, gm, pc, small)


def solution(mesh):
    N = int(round(mesh.shape["point"] ** 0.5))
    ND = mesh.shape["dp"]
    big = P("dp", "point", None)
    return jax.shard_map(
        functools.partial(per_device, N, ND),
        mesh=mesh,
        in_specs=(big, big, big, P(), P(), P()),
        out_specs=(big, big, big, P("dp", None), P("dp"), P("dp", None)),
        check_vma=False,
    )
```

```python
import functools

import jax
import jax.numpy as jnp
from jax import lax
from jax.experimental import pallas as pl
from jax.experimental.pallas import tpu as pltpu
from jax.sharding import PartitionSpec as P

epsilon = 1e-05
f32 = jnp.float32
bf16 = jnp.bfloat16
W = 64
Q = 4
QW = Q * W
BANDS = 1
VMEM_LIMIT = 40 * 1024 * 1024
NN = (((1,), (0,)), ((), ()))
NT = (((1,), (1,)), ((), ()))


def bdot(a, b, dims=NN):
    return lax.dot_general(a, b, dims, preferred_element_type=f32)


def hdot(a, b, dims=NN):
    ah, bh = a.astype(bf16), b.astype(bf16)
    al, bl = (a - ah.astype(f32)).astype(bf16), (b - bh.astype(f32)).astype(bf16)
    return bdot(ah, bh, dims) + (bdot(ah, bl, dims) + bdot(al, bh, dims))


def swap_halves(x):
    return pltpu.roll(x, W, 1)


def kernel(
    N,
    ND,
    H,
    node_h,
    pool_h,
    cot_h,
    w_h,
    sharp_h,
    maps_h,
    lo_ref,
    gm_ref,
    pc_ref,
    small_ref,
    node,
    pool,
    cot,
    w_ref,
    sharp_ref,
    maps_ref,
    zed,
    sl,
    slt,
    slb,
    glt,
    nodet,
    gpart,
    bt,
    mbs,
    gbs,
    send1,
    recv1,
    recv2,
    res,
    tpart,
    tgrad,
    fin,
    tred,
    fred,
    in_sem,
    par_sem,
    s1,
    r1,
    s2,
    r2,
    s3,
    r3,
    st,
    rt,
    sf,
    rf,
):
    QN = H // Q
    W2 = W // 2
    R = W // ND
    PTS = node.shape[0]
    point = lax.axis_index("point")
    me_d = lax.axis_index("dp")
    me_y = point // N
    me_z = point % N

    def first(f):
        return jnp.where(f == 0, me_y, me_z) if not isinstance(f, int) else (me_y, me_z)[f]

    def second(f):
        return jnp.where(f == 0, me_z, me_y) if not isinstance(f, int) else (me_z, me_y)[f]

    def place(f, i, j):
        if isinstance(f, int):
            return i * N + j if f == 0 else j * N + i
        return jnp.where(f == 0, i * N + j, j * N + i)

    def far_first(n):
        return sorted(range(1, n), key=lambda k: -min(k, n - k))

    def rcopy(src, dst, ssem, rsem, **dev):
        return pltpu.make_async_remote_copy(
            src_ref=src,
            dst_ref=dst,
            send_sem=ssem,
            recv_sem=rsem,
            device_id=dev,
            device_id_type=pl.DeviceIdType.MESH,
        )

    def wait_bytes(like, sem):
        pltpu.make_async_copy(like, like, sem).wait()

    barrier = pltpu.get_barrier_semaphore()

    def greet(**dev):
        pl.semaphore_signal(
            barrier, inc=1, device_id=dev, device_id_type=pl.DeviceIdType.MESH
        )

    def greet_ring(steps):
        for k in steps:
            greet(point=place(0, (me_y + k) % N, me_z))
            greet(point=place(0, me_y, (me_z + k) % N))

    greet_ring(far_first(N)[:3])

    inputs = [
        pltpu.make_async_copy(s.at[0], d, in_sem.at[n])
        for n, (s, d) in enumerate(((node_h, node), (pool_h, pool), (cot_h, cot)))
    ]
    params = [
        pltpu.make_async_copy(s, d, par_sem.at[n])
        for n, (s, d) in enumerate(((w_h, w_ref), (sharp_h, sharp_ref), (maps_h, maps_ref)))
    ]
    for c in params[:2] + inputs:
        c.start()
    greet_ring(far_first(N)[3:])
    for k in far_first(ND):
        greet(dp=(me_d + k) % ND)
    params[2].start()
    for c in params[:2]:
        c.wait()
    w4 = jnp.concatenate([w_ref[...].astype(f32)] * Q, axis=0)
    w4 = jnp.concatenate([w4] * Q, axis=1)
    row = lax.broadcasted_iota(jnp.int32, (QW, QW), 0)
    col = lax.broadcasted_iota(jnp.int32, (QW, QW), 1)
    w4 = jnp.where(row // W == col // W, w4, 0.0)
    bt[...] = w4.T.astype(bf16)
    low = lax.broadcasted_iota(jnp.int32, (W, 2 * W), 1) < W
    low2 = low[:W2]

    def inv_sharp(h, width):
        return 1.0 / jnp.full((1, width), sharp_ref[h], f32)

    def rows_of(q, i=0, n=QW):
        return pl.ds(pl.multiple_of(q * QW + i * W, W), n)

    def lanes_of(q):
        return pl.ds(pl.multiple_of(q * QW, QW), QW)

    def fold(x, i):
        if i % 2 == 0:
            return jnp.where(low2, x[:W2], swap_halves(x[W2:]))
        return jnp.where(low2, swap_halves(x[:W2]), x[W2:])

    def unfold(x):
        return jnp.concatenate([x[:, :W], swap_halves(x)[:, :W]], axis=0)

    def spread(x, i):
        other = swap_halves(x)
        up, down = (x, other) if i % 2 == 0 else (other, x)
        keep = low2 if i % 2 == 0 else ~low2
        return jnp.concatenate([jnp.where(keep, up, 0.0), jnp.where(keep, down, 0.0)], axis=0)

    def column(row):
        return jnp.broadcast_to(row, (8, 2 * W)).T[:, :1]

    rows_in = (W2 + 1, W2)
    rows_out = (W2, W2 + 1)

    def phase1(s, h, f, i):
        n = pl.ds(0, rows_in[s])
        return rcopy(
            send1.at[s, h, n],
            recv1.at[s, f, first(f), n],
            s1.at[s],
            r1.at[s],
            point=place(f, i, second(f)),
        )

    def soften(q, z):
        sums = []
        for i in range(Q):
            zh = z[i * W : (i + 1) * W] * inv_sharp(q * Q + i, PTS)
            e = jnp.exp(zh - jnp.max(zh, axis=0, keepdims=True))
            s = e * (1.0 / jnp.sum(e, axis=0, keepdims=True))
            sb = s.astype(bf16)
            zed[rows_of(q, i, W), :] = zh
            sl[rows_of(q, i, W), :] = s
            slt[rows_of(q, i, W), :] = sb
            sums.append(sum(s[:, c : c + 2 * W] for c in range(0, PTS, 2 * W)))
        return sums

    def gather(q, sums):
        sq = slt[rows_of(q), :]
        sums = jnp.concatenate(sums, axis=0)
        top = sums.astype(bf16)
        ones = jnp.ones((8, 2 * W), bf16)
        mass = bdot(ones, top, NT) + bdot(ones, (sums - top.astype(f32)).astype(bf16), NT)
        pooled = bdot(sq, pool[:, lanes_of(q)])
        gmixed = bdot(sq, cot[:, lanes_of(q)])
        for i in range(Q):
            r, c = slice(i * W, (i + 1) * W), slice(i // 2 * 2 * W, (i // 2 + 1) * 2 * W)
            m = mass[:, c] if i % 2 == 0 else swap_halves(mass[:, c])
            send1[0, q * Q + i, :W2, :] = fold(pooled[r, c], i)
            send1[0, q * Q + i, W2:, :] = m
            send1[1, q * Q + i, :W2, :] = fold(gmixed[r, c], i)


    inputs[0].wait()
    zs = [bdot(bt[...], node[:, lanes_of(q)], NT) for q in range(QN)]
    sums_of = [soften(q, zs[q]) for q in range(QN)]
    for c in inputs[1:]:
        c.wait()
    for q in range(QN):
        gather(q, sums_of[q])

    pl.semaphore_wait(barrier, 2 * (N - 1) + ND - 1)
    for s in range(2):
        for k in far_first(N):
            for f in range(2):
                i = (first(f) + k) % N
                phase1(s, f * N + i, f, i).start()

    for q in range(QN):
        slb[:, lanes_of(q)] = slt[rows_of(q), :].T
        nodet[rows_of(q), :] = node[:, lanes_of(q)].T
        mbs[q] = jnp.zeros((QW, QW), bf16)
        gbs[q] = jnp.zeros((QW, QW), bf16)

    def phase2(s, f, j):
        mine = recv2.at[s, f, second(f), pl.ds(0, rows_in[s])]
        return rcopy(
            mine, mine, s2.at[s], r2.at[s], point=place(f, first(f), j)
        )

    def arrived1(s):
        n = rows_in[s]
        for f in range(2):
            recv1[s, f, first(f)] = send1[s, f * N + first(f)]
        wait_bytes(recv1.at[s, :, pl.ds(0, N - 1), pl.ds(0, n)], r1.at[s])
        for f in range(2):
            part = recv1[s, f, 0, :n, :]
            for i in range(1, N):
                part = part + recv1[s, f, i, :n, :]
            recv2[s, f, second(f), :n, :] = part
        for k in far_first(N):
            for f in range(2):
                phase2(s, f, (second(f) + k) % N).start()

    def arrived2(s):
        n = rows_in[s]
        wait_bytes(recv2.at[s, :, pl.ds(0, N - 1), pl.ds(0, n)], r2.at[s])
        totals = []
        for f in range(2):
            total = recv2[s, f, 0, :n, :]
            for j in range(1, N):
                total = total + recv2[s, f, j, :n, :]
            totals.append(total)
        return totals

    for s in range(2):
        arrived1(s)

    params[2].wait()
    maps = maps_ref[...]

    def phase3(s, f, i):
        h = f * N + first(f)
        mine = res.at[s, h, pl.ds(0, rows_out[s])]
        return rcopy(
            mine, mine, s3.at[s], r3.at[s], point=place(f, i, second(f))
        )

    def send3(s):
        for k in far_first(N):
            for f in range(2):
                phase3(s, f, (first(f) + k) % N).start()

    totals = arrived2(0)
    mass = jnp.concatenate([total[W2:] for total in totals], axis=0)
    mass = jnp.concatenate([mass, jnp.ones((6, 2 * W), f32)], axis=0).T
    inverse = 1.0 / (jnp.concatenate([mass[:W, :1], mass[:W, 1:2]], axis=0) + epsilon)
    t = jnp.concatenate([unfold(total[:W2]) for total in totals], axis=0) * inverse
    proj = hdot(t, maps)
    query, key, value = proj[:, :W], swap_halves(proj[:, : 2 * W])[:, :W], proj[:, 2 * W :]
    score = hdot(query, key, NT) * W**-0.5
    row = lax.broadcasted_iota(jnp.int32, (2 * W, 2 * W), 0)
    col = lax.broadcasted_iota(jnp.int32, (2 * W, 2 * W), 1)
    score = jnp.where(row // W == col // W, score, -jnp.inf)
    e = jnp.exp(score - jnp.max(score, axis=1, keepdims=True))
    attn = e / jnp.sum(e, axis=1, keepdims=True)
    mixed = hdot(attn, value).astype(bf16).astype(f32)
    for f in range(2):
        res[0, f * N + first(f), :W2, :] = jnp.concatenate(
            [mixed[f * W : f * W + W2], mixed[f * W + W2 : (f + 1) * W]], axis=1
        )
    send3(0)

    gmix = jnp.concatenate([unfold(total) for total in arrived2(1)], axis=0)
    gattn = hdot(gmix, value, NT)
    gvalue = hdot(attn.T, gmix)
    gscore = attn * (gattn - jnp.sum(attn * gattn, axis=1, keepdims=True)) * W**-0.5
    gquery = hdot(gscore, key)
    gkey = hdot(gscore.T, query)
    gproj = jnp.concatenate([gquery, gkey, gvalue], axis=1)
    gtok = hdot(gvalue, maps[:, 2 * W :], NT) + hdot(gproj[:, : 2 * W], maps[:, : 2 * W], NT)
    gpool = (gtok * inverse).astype(bf16).astype(f32)
    gmass = hdot(jnp.ones((8, 3 * W), f32), -(gproj * proj) * inverse, NT)
    for f in range(2):
        h = f * N + first(f)
        res[1, h, :W2, :] = jnp.concatenate(
            [gpool[f * W : f * W + W2], gpool[f * W + W2 : (f + 1) * W]], axis=1
        )
        here, there = (gmass, swap_halves(gmass)) if f == 0 else (swap_halves(gmass), gmass)
        even = (jnp.zeros((8, 2 * W), jnp.int32) + h) % 2 == 0
        res[1, h, W2:, :] = jnp.where(
            even, jnp.where(low[:8], here, 0.0), jnp.where(low[:8], 0.0, there)
        )
    send3(1)

    def all_of(buf, ssem, rsem):
        axes = ((me_d, ND), (me_z, N), (me_y, N))

        def dev(stage, k):
            if stage == 0:
                return {"dp": k}
            return {"point": place(0, me_y, k) if stage == 1 else place(0, k, me_z)}

        def copy(stage, k, src):
            me = axes[stage][0]
            return rcopy(
                src, buf.at[stage, me], ssem.at[0], rsem.at[stage], **dev(stage, k)
            )

        def send(stage, source):
            me, n = axes[stage]
            for k in far_first(n):
                k = (me + k) % n
                copy(stage, k, source(k)).start()

        def receive(stage):
            me, n = axes[stage]
            wait_bytes(buf.at[stage, pl.ds(0, n - 1)], rsem.at[stage])
            total = buf[stage, 0]
            for k in range(1, n):
                total = total + buf[stage, k]
            return total

        def begin(source):
            buf[0, me_d] = source[me_d]
            send(0, lambda k: source.at[k])

        def onward(stage):
            total = receive(stage - 1)
            me = axes[stage][0]
            buf[stage, me] = total
            send(stage, lambda k: buf.at[stage, me])

        def finish():
            return receive(2)

        def drain():
            if N == ND:
                wait_bytes(buf.at[:, pl.ds(0, N - 1)], ssem.at[0])
            else:
                raise NotImplementedError

        return begin, onward, finish, drain

    t_begin, t_onward, t_finish, t_drain = all_of(tred, st, rt)
    f_begin, f_onward, f_finish, f_drain = all_of(fred, sf, rf)

    tg = hdot(t.T, gproj) * (1.0 / N)
    tg = jnp.concatenate([tg, jnp.zeros((W, W), f32)], axis=1)
    for d in range(ND):
        tgrad[d] = tg[d * R : (d + 1) * R]
    t_begin(tgrad)

    def await3(s):
        wait_bytes(res.at[s, pl.ds(0, 2 * N - 2), pl.ds(0, rows_out[s])], r3.at[s])

    def pair(i):
        return slice(i // 2 * 2 * W, (i // 2 + 1) * 2 * W)

    def with_mixed(groups):
        for q in groups:
            for i in range(Q):
                block = spread(res[0, q * Q + i, :W2, :], i)
                mbs[q, i * W : (i + 1) * W, pair(i)] = block.astype(bf16)
        for q in groups:
            gpart[rows_of(q), :] = bdot(mbs[q], cot[:, lanes_of(q)], NT)

    await3(0)
    with_mixed(range(QN))

    quarter = lax.broadcasted_iota(jnp.int32, (8, 2 * W), 1) // W2

    def backward(groups):
        gqs, cols = {}, {}
        for q in groups:
            cols[q] = []
            for i in range(Q):
                block = spread(res[1, q * Q + i, :W2, :], i)
                gbs[q, i * W : (i + 1) * W, pair(i)] = block.astype(bf16)
                if i % 2 == 0:
                    row = (
                        res[1, q * Q + i, W2 : W2 + 1, :] + res[1, q * Q + i + 1, W2 : W2 + 1, :]
                    )
                    cols[q].append(column(row))
        for q in groups:
            gqs[q] = gpart[rows_of(q), :] + bdot(gbs[q], pool[:, lanes_of(q)], NT)
        for q in groups:
            for i in range(Q):
                h = q * Q + i
                s = sl[rows_of(q, i, W), :]
                g = gqs[q][i * W : (i + 1) * W] + cols[q][i // 2][i % 2 * W : (i % 2 + 1) * W]
                sg = s * g
                gz = sg - s * jnp.sum(sg, axis=0, keepdims=True)
                glt[rows_of(q, i, W), :] = (gz * inv_sharp(h, PTS)).astype(bf16)
                tz = gz * zed[rows_of(q, i, W), :]
                tz = jnp.sum(tz.reshape(W // 8, 8, PTS), axis=0)
                tz = sum(tz[:, c : c + 2 * W] for c in range(0, PTS, 2 * W))
                tz = tz + swap_halves(tz)
                tz = (tz + pltpu.roll(tz, W2, 1)) * inv_sharp(h, 2 * W)
                part = jnp.where(quarter == 2 + i % 2, -tz, part if i % 2 else 0.0)
                if i % 2:
                    tpart[h // 2] = part
        sides = [0.0, 0.0]
        for q in groups:
            gs = bdot(nodet[rows_of(q), :], glt[rows_of(q), :], NT)
            for i in range(Q):
                sides[i % 2] = sides[i % 2] + gs[i * W : (i + 1) * W, pair(i)]
        return sides

    await3(1)
    left, right = backward(range(QN))

    gst = jnp.where(low, left + swap_halves(right), 0.0)
    for d in range(ND):
        fin[d] = gst[d * R : (d + 1) * R]
        fin[d, :8, :] = fin[d, :8, :] + tpart[d]
    f_begin(fin)

    def outputs(q):
        gl = glt[rows_of(q), :].T
        lo_ref[0, :, lanes_of(q)] = bdot(slb[:, lanes_of(q)], mbs[q]).astype(bf16)
        gm_ref[0, :, lanes_of(q)] = bdot(gl, bt[...]).astype(bf16)
        pc_ref[0, :, lanes_of(q)] = bdot(slb[:, lanes_of(q)], gbs[q]).astype(bf16)

    t_onward(1)
    for q in range(QN):
        outputs(q)
    f_onward(1)
    t_onward(2)
    for s in range(2):
        wait_bytes(send1.at[s, pl.ds(0, 2 * N - 2), pl.ds(0, rows_in[s])], s1.at[s])
        wait_bytes(recv2.at[s, :, pl.ds(0, N - 1), pl.ds(0, rows_in[s])], s2.at[s])
        wait_bytes(res.at[s, pl.ds(0, 2 * N - 2), pl.ds(0, rows_out[s])], s3.at[s])
    f_onward(2)
    small_ref[:, 2 * W :] = t_finish()
    t_drain()
    small_ref[:, : 2 * W] = f_finish()
    f_drain()


def finish_kernel(
    lo_i,
    gm_i,
    pc_i,
    small,
    lo_h,
    gm_h,
    pc_h,
    gs_h,
    gt_h,
    gk_h,
    gs,
    gk,
    gt,
    sem,
):
    rows = lo_i.shape[1] // BANDS
    pairs = [(gs, gs_h), (gk, gk_h), (gt, gt_h)]
    for p in range(BANDS):
        band = (0, pl.ds(p * rows, rows))
        pairs += [(s.at[band], d.at[band]) for s, d in ((lo_i, lo_h), (gm_i, gm_h), (pc_i, pc_h))]
    copies = [pltpu.make_async_copy(s, d, sem.at[n]) for n, (s, d) in enumerate(pairs)]
    for c in copies[3:]:
        c.start()
    gs[...] = small[:, :W]
    gk[...] = small[:, 2 * W : 5 * W]
    quarter = lax.broadcasted_iota(jnp.int32, (8, 2 * W), 1) // (W // 2)
    for n in range(2):
        gt[n] = jnp.sum(jnp.where(quarter == 2 + n, small[:8, : 2 * W], 0.0))
    for c in copies[:3]:
        c.start()
    for c in copies:
        c.wait()


def per_device(N, ND, node, pool, cot, w, sharp, maps):
    _, pts, width = node.shape
    H = sharp.shape[0]
    QN = H // Q
    W2 = W // 2
    R = W // ND
    any_ = pl.BlockSpec(memory_space=pl.ANY)
    vmem = pl.BlockSpec(memory_space=pltpu.VMEM)
    big = jax.ShapeDtypeStruct((1, pts, width), bf16)
    dma = pltpu.SemaphoreType.DMA
    node, pool, cot, w, sharp, maps = (
        pltpu.with_memory_space_constraint(a, pltpu.HBM) for a in (node, pool, cot, w, sharp, maps)
    )
    lo, gm, pc, small = pl.pallas_call(
        functools.partial(kernel, N, ND, H),
        out_shape=(big, big, big, jax.ShapeDtypeStruct((R, 6 * W), f32)),
        in_specs=[any_] * 6,
        out_specs=[vmem] * 4,
        scratch_shapes=[
            pltpu.VMEM((pts, width), bf16),
            pltpu.VMEM((pts, width), bf16),
            pltpu.VMEM((pts, width), bf16),
            pltpu.VMEM((W, W), bf16),
            pltpu.SMEM((H,), f32),
            pltpu.VMEM((W, 3 * W), f32),
            pltpu.VMEM((width, pts), f32),
            pltpu.VMEM((width, pts), f32),
            pltpu.VMEM((width, pts), bf16),
            pltpu.VMEM((pts, width), bf16),
            pltpu.VMEM((width, pts), bf16),
            pltpu.VMEM((width, pts), bf16),
            pltpu.VMEM((width, pts), f32),
            pltpu.VMEM((QW, QW), bf16),
            pltpu.VMEM((QN, QW, QW), bf16),
            pltpu.VMEM((QN, QW, QW), bf16),
            pltpu.VMEM((2, H, W2 + 8, 2 * W), f32),
            pltpu.VMEM((2, 2, N, W2 + 8, 2 * W), f32),
            pltpu.VMEM((2, 2, N, W2 + 8, 2 * W), f32),
            pltpu.VMEM((2, H, W2 + 8, 2 * W), f32),
            pltpu.VMEM((H // 2, 8, 2 * W), f32),
            pltpu.VMEM((ND, R, 4 * W), f32),
            pltpu.VMEM((ND, R, 2 * W), f32),
            pltpu.VMEM((3, max(N, ND), R, 4 * W), f32),
            pltpu.VMEM((3, max(N, ND), R, 2 * W), f32),
            dma((3,)),
            dma((3,)),
            dma((2,)),
            dma((2,)),
            dma((2,)),
            dma((2,)),
            dma((2,)),
            dma((2,)),
            dma((1,)),
            dma((3,)),
            dma((1,)),
            dma((3,)),
        ],
        compiler_params=pltpu.CompilerParams(
            collective_id=0, has_side_effects=True, vmem_limit_bytes=VMEM_LIMIT
        ),
    )(node, pool, cot, w, sharp, maps)
    each = H // ND
    return pl.pallas_call(
        finish_kernel,
        out_shape=(
            big,
            big,
            big,
            jax.ShapeDtypeStruct((R, W), f32),
            jax.ShapeDtypeStruct((each,), f32),
            jax.ShapeDtypeStruct((R, 3 * W), f32),
        ),
        in_specs=[vmem] * 4,
        out_specs=[any_] * 6,
        scratch_shapes=[
            pltpu.VMEM((R, W), f32),
            pltpu.VMEM((R, 3 * W), f32),
            pltpu.SMEM((each,), f32),
            dma((3 + 3 * BANDS,)),
        ],
        compiler_params=pltpu.CompilerParams(vmem_limit_bytes=VMEM_LIMIT),
    )(lo, gm, pc, small)


def solution(mesh):
    N = int(round(mesh.shape["point"] ** 0.5))
    ND = mesh.shape["dp"]
    big = P("dp", "point", None)
    return jax.shard_map(
        functools.partial(per_device, N, ND),
        mesh=mesh,
        in_specs=(big, big, big, P(), P(), P()),
        out_specs=(big, big, big, P("dp", None), P("dp"), P("dp", None)),
        check_vma=False,
    )
```
